256 devices in a mesh: slab: 32 (over z, x), src: 8 (over y, core).
Axes of the slice: x: 4, y: 4, z: 8, core: 2. Of those that a mesh axis runs over, the one named last changes fastest.
Arguments:
- sigma: float32 [128, 128, 128], P('slab'), may hold values from 0.2 to 2
- iterate: float32 [32, 128, 128, 128], P('src', 'slab'), may hold values from -4.5 to 4.5, as said below
- counts: int32 [8], replicated, may hold values from 0 to 4, as said below
- sources: int32 [8, 4], replicated, may hold values from 0 to 2097151
Outputs:
- potential: float32 [32, 128, 128, 128], P('src', 'slab')
- residual: float32 [32, 128, 128, 128], P('src', 'slab')
The draws below stay inside these ranges and needn't reach their ends.
Inputs may be any that keep to these rules, and one draw needn't show every extreme that they name: counts[g] + counts[(g + 4) % 8] = 4 for every group g, and some group holds 4 live columns in every draw. `iterate`: rough values.
All inputs are finite; a program needn't handle non-finite values.
Results may differ from the reference program's by a relative error of at most 0.0003.
Values sent between devices are 32-bit elements; how exact they have to be, the bound alone decides.
A program may use at most 64 MiB of HBM per device.

```python
import math
from functools import reduce
import jax
import jax.numpy as jnp
from jax import lax

NX = 128
NY = 128
MAXC = 4
BAL = 2
ITERS = 6
NZ = 128
NGROUP = 8
SLOTS = 32
CELLS = 2097152


def draw_counts(key, part):
    half = NGROUP // 2
    offsets = jax.random.randint(jax.random.fold_in(key, 12), (half,), 1, 3)
    first = jax.random.randint(jax.random.fold_in(key, 13), (), 0, half)
    offsets = jnp.where(jnp.arange(half) == first, 2, offsets)
    signs = 2 * jax.random.randint(jax.random.fold_in(key, 14), (half,), 0, 2) - 1
    moved = offsets * signs
    values = jnp.concatenate([BAL + moved, BAL - moved]).astype(jnp.int32)
    return values


def draw_iterate(key, part):
    shape = (SLOTS, NZ, NX, NY)
    values = jnp.clip(1.5 * jax.random.normal(jax.random.fold_in(key, 22), shape, jnp.float32), -4.5, 4.5)
    return values.astype(jnp.float32)


def set_ends(drawn, key, least, high):
    longest = drawn.shape.index(max(drawn.shape))
    spots = []
    for shift in (0, 1):
        where = [jax.random.randint(jax.random.fold_in(key, axis), (), 0, length) for axis, length in enumerate(drawn.shape)]
        where[longest] = (where[longest] + shift) % drawn.shape[longest]
        spots.append(tuple(where))
    return drawn.at[spots[0]].set(least).at[spots[1]].set(high)


def steps_of(stream_key, shape, shards, low, high):
    factor_of, own = 1.0, jax.random.fold_in(stream_key, 6)
    for position, blocks in shards:
        steps = jnp.exp(jax.random.uniform(jax.random.fold_in(own, position), (blocks,), jnp.float32, low / len(shards), high / len(shards)))
        factor_of = factor_of * jnp.repeat(steps, shape[position] // blocks).reshape([-1 if axis == position else 1 for axis in range(len(shape))])
    return factor_of


def setup_inputs(seed: int = 0) -> dict:
    keys = jax.random.split(jax.random.key(seed), 5)
    return {
        "sigma": jnp.clip(jnp.exp(math.log(2.0) - 2.3025851 * jax.random.uniform(keys[0], (NZ, NX, NY), jnp.float32) ** steps_of(keys[0], (NZ, NX, NY), ((0, 32),), -0.2, 0.2)), 0.2, 2.0),
        "iterate": draw_iterate(jax.random.fold_in(keys[4], 71), 0),
        "counts": draw_counts(jax.random.fold_in(keys[4], 71), 0),
        "sources": set_ends(jax.random.randint(keys[3], (NGROUP, MAXC), 0, CELLS), jax.random.fold_in(keys[3], 1), 0, CELLS - 1).astype(jnp.int32),
    }


def face(first, second):
    return 2.0 * first * second / (first + second)


def coefficients(sigma):
    padded = jnp.pad(sigma, 1, mode="edge")
    neighbours = (padded[:-2, 1:-1, 1:-1], padded[2:, 1:-1, 1:-1], padded[1:-1, :-2, 1:-1], padded[1:-1, 2:, 1:-1], padded[1:-1, 1:-1, :-2], padded[1:-1, 1:-1, 2:])
    weights = tuple(face(sigma, other) for other in neighbours)
    diag = reduce(lambda left, right: left + right, weights)
    return weights, diag


def operate(field, weights, diag):
    padded = jnp.pad(field, 1)
    neighbours = (padded[:-2, 1:-1, 1:-1], padded[2:, 1:-1, 1:-1], padded[1:-1, :-2, 1:-1], padded[1:-1, 2:, 1:-1], padded[1:-1, 1:-1, :-2], padded[1:-1, 1:-1, 2:])
    terms = [weight * other for weight, other in zip(weights, neighbours)]
    return diag * field - reduce(lambda left, right: left + right, terms)


def reference(sigma, iterate, counts, sources):
    weights, diag = coefficients(sigma)
    cell_ids = jnp.arange(NZ * NX * NY, dtype=jnp.int32).reshape(NZ, NX, NY)
    flat_sources = sources.reshape(-1)

    def solve_slot(item):
        start_x, slot = item
        group = slot // MAXC
        place = slot % MAXC
        live = place < counts[group]
        rhs = (cell_ids == flat_sources[slot]).astype(jnp.float32)
        x_now = start_x
        r_now = rhs - operate(x_now, weights, diag)
        z_now = r_now / diag
        p_now = z_now
        rz_now = jnp.sum(r_now * z_now)
        for step in range(ITERS):
            image = operate(p_now, weights, diag)
            alpha = rz_now / jnp.sum(p_now * image)
            x_now = x_now + alpha * p_now
            r_now = r_now - alpha * image
            z_now = r_now / diag
            rz_new = jnp.sum(r_now * z_now)
            p_now = z_now + (rz_new / rz_now) * p_now
            rz_now = rz_new
        return jnp.where(live, x_now, start_x), jnp.where(live, r_now, jnp.zeros_like(r_now))

    potential, residual = lax.map(solve_slot, (iterate, jnp.arange(SLOTS, dtype=jnp.int32)))
    return potential, residual
```

```python
import functools

import jax
import jax.numpy as jnp
from jax import lax
from jax.experimental import pallas as pl
from jax.experimental.pallas import tpu as pltpu
from jax.sharding import PartitionSpec as P

MESH = pl.DeviceIdType.MESH
ITERS = 6
STAGES = ITERS + 1
RING = 4
PAD = 8
CHUNK = 32

A = (-0.1666, -0.13, -0.07, -0.02, -0.02, -0.01)
B = (0.0, 0.373, 0.458, 0.484, 0.487, 0.493, 0.495)

PAIRS = [(i, j) for j in range(STAGES) for i in range(min(j + 1, ITERS))]
SLOT = {pair: at for at, pair in enumerate(PAIRS)}


def face(first, second):
    return 2.0 * first * second / (first + second)


def coefficients(gram):
    zero = jnp.zeros_like(gram(0, 0))
    one = zero + 1.0
    c_r, c_p = [one], [one]
    c_x = [zero] * ITERS
    r_dot = [gram(0, l) for l in range(STAGES)]
    rz = r_dot[0]
    for step in range(ITERS):
        c_q = [zero] * (step + 2)
        for i in range(step + 1):
            c_q[i] = c_q[i] + (1.0 - A[i]) * c_p[i]
            c_q[i + 1] = c_q[i + 1] - B[i + 1] * c_p[i]
            if i:
                c_q[i - 1] = c_q[i - 1] - B[i] * c_p[i]
        q_dot = {
            l: functools.reduce(lambda s, t: s + t, [c_q[i] * gram(i, l) for i in range(step + 2)])
            for l in range(step, ITERS)
        }
        alpha = rz / (c_r[step] * q_dot[step])
        c_x = [c_x[i] + alpha * c_p[i] if i <= step else c_x[i] for i in range(ITERS)]
        c_r = [(c_r[i] if i <= step else zero) - alpha * c_q[i] for i in range(step + 2)]
        if step + 1 < ITERS:
            r_dot = {l: r_dot[l] - alpha * q_dot[l] for l in range(step + 1, ITERS)}
            rz_new = c_r[step + 1] * r_dot[step + 1]
            beta = rz_new / rz
            rz = rz_new
            c_p = [c_r[i] + (beta * c_p[i] if i <= step else zero) for i in range(step + 2)]
    return c_x, c_r


def kernel(
    dims,
    counts, sources, sigma_hbm, x_hbm, pot_hbm, res_hbm,
    sig, x_in, v, halo, sig_halo, weights, diag, recip, rows_acc, x_parts, z_parts, table, pot, res,
    load_sem, out_sem, sig_send, sig_recv, send_sem, recv_sem, xs_send, xs_recv, zs_send, zs_recv,
):
    slabs, ncol, depth, rows = dims
    zs = slabs // RING
    cells = depth * rows
    plane = rows
    slab = lax.axis_index("slab")
    group = lax.axis_index("src")
    here_z, here_x = slab // RING, slab % RING
    left, right = (slab + slabs - 1) % slabs, (slab + 1) % slabs

    def peer(at):
        return (at, group)

    x_peers = [here_z * RING + (here_x + d) % RING for d in range(1, RING)]
    z_peers = [((here_z + d) % zs) * RING + here_x for d in range(1, zs)]
    body = pl.ds(PAD, cells)

    load_sig = pltpu.make_async_copy(sigma_hbm, sig.at[body], load_sem.at[0])
    load_sig.start()
    load_x = [pltpu.make_async_copy(x_hbm.at[c], x_in.at[c, body], load_sem.at[1 + c]) for c in range(ncol)]
    for copy in load_x:
        copy.start()

    barrier = pltpu.get_barrier_semaphore()
    greeted = [left, right] + x_peers + z_peers
    for at in greeted:
        pl.semaphore_signal(barrier, inc=1, device_id=peer(at), device_id_type=MESH)
    pl.semaphore_wait(barrier, len(greeted))

    low_rows, high_rows = pl.ds(0, plane), pl.ds(cells - plane, plane)

    def remote(src, dst, send, recv, at):
        return pltpu.make_async_remote_copy(
            src_ref=src, dst_ref=dst, send_sem=send, recv_sem=recv, device_id=peer(at), device_id_type=MESH
        )

    sig_copies = [
        remote(sigma_hbm.at[high_rows], sig_halo.at[0], sig_send.at[0], sig_recv.at[0], right),
        remote(sigma_hbm.at[low_rows], sig_halo.at[1], sig_send.at[1], sig_recv.at[1], left),
    ]
    for copy in sig_copies:
        copy.start()

    def halo_copies(k, c):
        if k == 0:
            high, low = x_hbm.at[c, high_rows], x_hbm.at[c, low_rows]
        else:
            high = v.at[k - 1, c, pl.ds(PAD + cells - plane, plane)]
            low = v.at[k - 1, c, pl.ds(PAD, plane)]
        return (
            remote(high, halo.at[k, 0, c], send_sem.at[k, 0, c], recv_sem.at[k, 0, c], right),
            remote(low, halo.at[k, 1, c], send_sem.at[k, 1, c], recv_sem.at[k, 1, c], left),
        )

    for c in range(ncol):
        for copy in halo_copies(0, c):
            copy.start()

    blank = jnp.zeros((PAD, 128), jnp.float32)
    for c in range(ncol):
        x_in[c, pl.ds(0, PAD)] = blank
        x_in[c, pl.ds(PAD + cells, PAD)] = blank
        for k in range(STAGES):
            v[k, c, pl.ds(0, PAD)] = blank
            v[k, c, pl.ds(PAD + cells, PAD)] = blank
    sig[pl.ds(0, PAD)] = blank + 1.0
    sig[pl.ds(PAD + cells, PAD)] = blank + 1.0
    rows_acc[...] = jnp.zeros_like(rows_acc)

    load_sig.wait()
    for copy in sig_copies:
        copy.wait_recv()

    lane = lax.broadcasted_iota(jnp.int32, (CHUNK, 128), 1)
    sub = lax.broadcasted_iota(jnp.int32, (CHUNK, 128), 0)
    per_plane = plane // CHUNK

    def start_row(q):
        return pl.multiple_of(q * CHUNK, CHUNK)

    def make_weights(row, below, above, open_below, open_above):
        own = sig[pl.ds(PAD + row, CHUNK)]
        x_at = sub + row % plane
        first_x, last_x = x_at == 0, x_at == plane - 1
        first_y, last_y = lane == 0, lane == 127
        others = (
            (below, open_below),
            (above, open_above),
            (sig[pl.ds(PAD - 1 + row, CHUNK)], first_x),
            (sig[pl.ds(PAD + 1 + row, CHUNK)], last_x),
            (pltpu.roll(own, 1, 1), first_y),
            (pltpu.roll(own, 127, 1), last_y),
        )
        total = None
        inner = []
        for other, outside in others:
            w = face(own, jnp.where(outside, own, other))
            total = w if total is None else total + w
            inner.append(jnp.where(outside, 0.0, w))
        inverse = 1.0 / total
        at = pl.ds(row, CHUNK)
        diag[at] = total
        recip[at] = inverse
        for i, w in enumerate(inner):
            weights[i, at] = w * inverse

    def weight_chunk(z, q):
        row = start_row(z * per_plane + q)
        local = pl.ds(start_row(q), CHUNK)
        below = sig_halo[0, local] if z == 0 else sig[pl.ds(PAD + row - plane, CHUNK)]
        above = sig_halo[1, local] if z == depth - 1 else sig[pl.ds(PAD + row + plane, CHUNK)]
        first = (slab == 0) if z == 0 else False
        last = (slab == slabs - 1) if z == depth - 1 else False
        never = jnp.zeros((CHUNK, 128), jnp.int32)
        open_below = (never + first.astype(jnp.int32)) > 0 if z == 0 else never > 0
        open_above = (never + last.astype(jnp.int32)) > 0 if z == depth - 1 else never > 0
        make_weights(row, below, above, open_below, open_above)

    for z in range(depth):
        lax.fori_loop(0, per_plane, lambda q, _, z=z: (weight_chunk(z, q), 0)[1], 0)

    def stage(k, c):
        def field(at):
            return x_in[c, at] if k == 0 else v[k - 1, c, at]

        cell = sources[group, c] - slab * (cells * 128) if k == 0 else None

        def chunk(row, below, above):
            here = pl.ds(PAD + row, CHUNK)
            at = pl.ds(row, CHUNK)
            mid = field(here)
            image = (
                weights[0, at] * below
                + weights[1, at] * above
                + weights[2, at] * field(pl.ds(PAD - 1 + row, CHUNK))
                + weights[3, at] * field(pl.ds(PAD + 1 + row, CHUNK))
                + weights[4, at] * pltpu.roll(mid, 1, 1)
                + weights[5, at] * pltpu.roll(mid, 127, 1)
            )
            if k == 0:
                ids = (sub + row) * 128 + lane
                new = jnp.where(ids == cell, recip[at], 0.0) + (image - mid)
            else:
                j = k - 1
                new = (1.0 / B[k]) * image + (-A[j] / B[k]) * mid
                if j:
                    new = new + (-B[j] / B[k]) * v[k - 2, c, here]
            v[k, c, here] = new

        def edge(q, _):
            row = start_row(q)
            chunk(row, halo[k, 0, c, pl.ds(row, CHUNK)], field(pl.ds(PAD + row + plane, CHUNK)))
            top = start_row(q + (depth - 1) * per_plane)
            chunk(top, field(pl.ds(PAD + top - plane, CHUNK)), halo[k, 1, c, pl.ds(row, CHUNK)])
            return 0

        lax.fori_loop(0, per_plane, edge, 0)
        if k < ITERS:
            for copy in halo_copies(k + 1, c):
                copy.start()

        def inside(q, _):
            row = start_row(q)
            chunk(row, field(pl.ds(PAD + row - plane, CHUNK)), field(pl.ds(PAD + row + plane, CHUNK)))
            return 0

        lax.fori_loop(per_plane, (depth - 1) * per_plane, inside, 0)

        def dots(q, sums):
            row = start_row(q)
            here = pl.ds(PAD + row, CHUNK)
            scaled = diag[pl.ds(row, CHUNK)] * v[k, c, here]
            out = []
            for i, total in enumerate(sums):
                product = scaled * v[i, c, here]
                for part in range(CHUNK // 8):
                    total = total + product[part * 8:(part + 1) * 8]
                out.append(total)
            return tuple(out)

        count = min(k + 1, ITERS)
        sums = lax.fori_loop(
            0, depth * per_plane, dots, tuple(jnp.zeros((8, 128), jnp.float32) for _ in range(count))
        )
        for i, total in enumerate(sums):
            rows_acc[pl.ds(SLOT[i, k] * ncol + c, 1), :] = jnp.sum(total, axis=0, keepdims=True)

    for k in range(STAGES):
        def column(c, _, k=k):
            if k == 0:
                pltpu.make_async_copy(x_hbm.at[c], x_in.at[c, body], load_sem.at[1 + c]).wait()
            for copy in halo_copies(k, c):
                copy.wait_recv()
            stage(k, c)
            return 0

        lax.fori_loop(0, ncol, column, 0)

    mine = jnp.sum(jnp.transpose(rows_acc[...]), axis=0, keepdims=True)
    x_parts[here_x] = mine
    x_copies = [
        remote(x_parts.at[here_x], x_parts.at[here_x], xs_send.at[d], xs_recv.at[d], at)
        for d, at in enumerate(x_peers)
    ]
    for copy in x_copies:
        copy.start()
    for copy in x_copies:
        copy.wait_recv()
    total = x_parts[0]
    for i in range(1, RING):
        total = total + x_parts[i]
    z_parts[here_z] = total
    z_copies = [
        remote(z_parts.at[here_z], z_parts.at[here_z], zs_send.at[d], zs_recv.at[d], at)
        for d, at in enumerate(z_peers)
    ]
    for copy in z_copies:
        copy.start()
    for copy in z_copies:
        copy.wait_recv()
    total = z_parts[0]
    for i in range(1, zs):
        total = total + z_parts[i]

    wide = jnp.broadcast_to(total, (8, 128))
    entries = {}
    for pair, at in SLOT.items():
        entries[pair] = wide if at == 0 else pltpu.roll(wide, 128 - at * ncol, 1)

    def gram(i, j):
        return entries[(i, j)] if i <= j and (i, j) in entries else entries[(j, i)]

    c_x, c_r = coefficients(gram)
    live = lax.broadcasted_iota(jnp.int32, (8, 128), 1) < counts[group]
    for j, value in enumerate(c_x + c_r):
        value = jnp.where(live, value, 0.0)
        for c in range(ncol):
            table[c, pl.ds(j, 1)] = jnp.broadcast_to(value[:1, c:c + 1], (1, 128))

    for c in range(ncol):
        def combine(q, _, c=c):
            row = start_row(q)
            here, at = pl.ds(PAD + row, CHUNK), pl.ds(row, CHUNK)
            new_x, new_r = x_in[c, here], None
            for j in range(STAGES):
                vec = v[j, c, here]
                if j < ITERS:
                    new_x = new_x + table[c, pl.ds(j, 1)] * vec
                term = table[c, pl.ds(ITERS + j, 1)] * vec
                new_r = term if new_r is None else new_r + term
            pot[c, at] = new_x
            res[c, at] = diag[at] * new_r
            return 0

        lax.fori_loop(0, depth * per_plane, combine, 0)
        pltpu.make_async_copy(pot.at[c], pot_hbm.at[c], out_sem.at[0, c]).start()
        pltpu.make_async_copy(res.at[c], res_hbm.at[c], out_sem.at[1, c]).start()

    for copy in sig_copies + x_copies + z_copies:
        copy.wait_send()
    for k in range(STAGES):
        for c in range(ncol):
            for copy in halo_copies(k, c):
                copy.wait_send()
    for c in range(ncol):
        pltpu.make_async_copy(pot.at[c], pot_hbm.at[c], out_sem.at[0, c]).wait()
        pltpu.make_async_copy(res.at[c], res_hbm.at[c], out_sem.at[1, c]).wait()


def solution(mesh):
    slabs = mesh.shape["slab"]

    def shards(sigma, iterate, counts, sources):
        depth, rows, lanes = sigma.shape
        ncol = iterate.shape[0]
        cells = depth * rows
        f32 = jnp.float32
        vmem = pltpu.VMEM
        dma = pltpu.SemaphoreType.DMA
        zs = slabs // RING
        flat = jax.ShapeDtypeStruct((ncol, cells, lanes), f32)
        potential, residual = pl.pallas_call(
            functools.partial(kernel, (slabs, ncol, depth, rows)),
            out_shape=(flat, flat),
            in_specs=[
                pl.BlockSpec(memory_space=pltpu.SMEM),
                pl.BlockSpec(memory_space=pltpu.SMEM),
                pl.BlockSpec(memory_space=pl.ANY),
                pl.BlockSpec(memory_space=pl.ANY),
            ],
            out_specs=(pl.BlockSpec(memory_space=pl.ANY), pl.BlockSpec(memory_space=pl.ANY)),
            scratch_shapes=[
                vmem((cells + 2 * PAD, lanes), f32),
                vmem((ncol, cells + 2 * PAD, lanes), f32),
                vmem((STAGES, ncol, cells + 2 * PAD, lanes), f32),
                vmem((STAGES, 2, ncol, rows, lanes), f32),
                vmem((2, rows, lanes), f32),
                vmem((6, cells, lanes), f32),
                vmem((cells, lanes), f32),
                vmem((cells, lanes), f32),
                vmem((128, 128), f32),
                vmem((RING, 1, 128), f32),
                vmem((zs, 1, 128), f32),
                vmem((ncol, 16, 128), f32),
                vmem((ncol, cells, lanes), f32),
                vmem((ncol, cells, lanes), f32),
                dma((1 + ncol,)),
                dma((2, ncol)),
                dma((2,)),
                dma((2,)),
                dma((STAGES, 2, ncol)),
                dma((STAGES, 2, ncol)),
                dma((RING - 1,)),
                dma((RING - 1,)),
                dma((zs - 1,)),
                dma((zs - 1,)),
            ],
            compiler_params=pltpu.CompilerParams(
                collective_id=0, has_side_effects=True, vmem_limit_bytes=40 * 1024 * 1024
            ),
        )(counts, sources, sigma.reshape(cells, lanes), iterate.reshape(ncol, cells, lanes))
        return potential.reshape(iterate.shape), residual.reshape(iterate.shape)

    return jax.shard_map(
        shards,
        mesh=mesh,
        in_specs=(P("slab", None, None), P("src", "slab", None, None), P(), P()),
        out_specs=(P("src", "slab", None, None), P("src", "slab", None, None)),
        check_vma=False,
    )
```

```python
import functools

import jax
import jax.numpy as jnp
from jax import lax
from jax.experimental import pallas as pl
from jax.experimental.pallas import tpu as pltpu
from jax.sharding import PartitionSpec as P

MESH = pl.DeviceIdType.MESH
ITERS = 6
STAGES = ITERS + 1
RING = 4
PAD = 8
CHUNK = 64

A = (-0.1666, -0.13, -0.07, -0.02, -0.02, -0.01)
B = (0.0, 0.373, 0.458, 0.484, 0.487, 0.493, 0.495)

PAIRS = [(i, j) for j in range(STAGES) for i in range(min(j + 1, ITERS))]
SLOT = {pair: at for at, pair in enumerate(PAIRS)}


def face(first, second):
    return 2.0 * first * second / (first + second)


def coefficients(gram):
    zero = jnp.zeros_like(gram(0, 0))
    one = zero + 1.0
    c_r, c_p = [one], [one]
    c_x = [zero] * ITERS
    r_dot = [gram(0, l) for l in range(STAGES)]
    rz = r_dot[0]
    for step in range(ITERS):
        c_q = [zero] * (step + 2)
        for i in range(step + 1):
            c_q[i] = c_q[i] + (1.0 - A[i]) * c_p[i]
            c_q[i + 1] = c_q[i + 1] - B[i + 1] * c_p[i]
            if i:
                c_q[i - 1] = c_q[i - 1] - B[i] * c_p[i]
        q_dot = {
            l: functools.reduce(lambda s, t: s + t, [c_q[i] * gram(i, l) for i in range(step + 2)])
            for l in range(step, ITERS)
        }
        alpha = rz / (c_r[step] * q_dot[step])
        c_x = [c_x[i] + alpha * c_p[i] if i <= step else c_x[i] for i in range(ITERS)]
        c_r = [(c_r[i] if i <= step else zero) - alpha * c_q[i] for i in range(step + 2)]
        if step + 1 < ITERS:
            r_dot = {l: r_dot[l] - alpha * q_dot[l] for l in range(step + 1, ITERS)}
            rz_new = c_r[step + 1] * r_dot[step + 1]
            beta = rz_new / rz
            rz = rz_new
            c_p = [c_r[i] + (beta * c_p[i] if i <= step else zero) for i in range(step + 2)]
    return c_x, c_r


def basis_kernel(
    dims,
    counts_hbm, sources_hbm, sigma_hbm, x_hbm, x_in, v, diag, table,
    counts, sources, sig, halo, sig_halo, weights, recip, rows_acc, x_parts, z_parts,
    load_sem, sig_send, sig_recv, send_sem, recv_sem, xs_send, xs_recv, zs_send, zs_recv,
):
    slabs, ncol, depth, rows = dims
    zs = slabs // RING
    cells = depth * rows
    plane = rows
    slab = lax.axis_index("slab")
    group = lax.axis_index("src")
    here_z, here_x = slab // RING, slab % RING
    left, right = (slab + slabs - 1) % slabs, (slab + 1) % slabs

    def peer(at):
        return (at, group)

    x_peers = [here_z * RING + (here_x + d) % RING for d in range(1, RING)]
    z_peers = [((here_z + d) % zs) * RING + here_x for d in range(1, zs)]
    body = pl.ds(PAD, cells)

    load_sig = pltpu.make_async_copy(sigma_hbm, sig.at[body], load_sem.at[0])
    load_sig.start()
    load_x = [pltpu.make_async_copy(x_hbm.at[c], x_in.at[c, body], load_sem.at[1 + c]) for c in range(ncol)]
    for copy in load_x:
        copy.start()
    load_ints = [
        pltpu.make_async_copy(counts_hbm, counts, load_sem.at[1 + ncol]),
        pltpu.make_async_copy(sources_hbm, sources, load_sem.at[2 + ncol]),
    ]
    for copy in load_ints:
        copy.start()

    barrier = pltpu.get_barrier_semaphore()
    greeted = [left, right] + x_peers + z_peers
    for at in greeted:
        pl.semaphore_signal(barrier, inc=1, device_id=peer(at), device_id_type=MESH)
    pl.semaphore_wait(barrier, len(greeted))

    low_rows, high_rows = pl.ds(0, plane), pl.ds(cells - plane, plane)

    def remote(src, dst, send, recv, at):
        return pltpu.make_async_remote_copy(
            src_ref=src, dst_ref=dst, send_sem=send, recv_sem=recv, device_id=peer(at), device_id_type=MESH
        )

    sig_copies = [
        remote(sigma_hbm.at[high_rows], sig_halo.at[0], sig_send.at[0], sig_recv.at[0], right),
        remote(sigma_hbm.at[low_rows], sig_halo.at[1], sig_send.at[1], sig_recv.at[1], left),
    ]
    for copy in sig_copies:
        copy.start()

    def halo_copies(k, c):
        if k == 0:
            high, low = x_hbm.at[c, high_rows], x_hbm.at[c, low_rows]
        else:
            high = v.at[k - 1, c, pl.ds(PAD + cells - plane, plane)]
            low = v.at[k - 1, c, pl.ds(PAD, plane)]
        return (
            remote(high, halo.at[k, 0, c], send_sem.at[k, 0, c], recv_sem.at[k, 0, c], right),
            remote(low, halo.at[k, 1, c], send_sem.at[k, 1, c], recv_sem.at[k, 1, c], left),
        )

    for c in range(ncol):
        for copy in halo_copies(0, c):
            copy.start()

    blank = jnp.zeros((PAD, 128), jnp.float32)
    for c in range(ncol):
        x_in[c, pl.ds(0, PAD)] = blank
        x_in[c, pl.ds(PAD + cells, PAD)] = blank
        for k in range(STAGES):
            v[k, c, pl.ds(0, PAD)] = blank
            v[k, c, pl.ds(PAD + cells, PAD)] = blank
    sig[pl.ds(0, PAD)] = blank + 1.0
    sig[pl.ds(PAD + cells, PAD)] = blank + 1.0
    rows_acc[...] = jnp.zeros_like(rows_acc)

    load_sig.wait()

    lane = lax.broadcasted_iota(jnp.int32, (CHUNK, 128), 1)
    sub = lax.broadcasted_iota(jnp.int32, (CHUNK, 128), 0)
    per_plane = plane // CHUNK

    def start_row(q):
        return pl.multiple_of(q * CHUNK, CHUNK)

    def make_weights(row, below, above, open_below, open_above):
        own = sig[pl.ds(PAD + row, CHUNK)]
        x_at = sub + row % plane
        first_x, last_x = x_at == 0, x_at == plane - 1
        first_y, last_y = lane == 0, lane == 127
        others = (
            (below, open_below),
            (above, open_above),
            (sig[pl.ds(PAD - 1 + row, CHUNK)], first_x),
            (sig[pl.ds(PAD + 1 + row, CHUNK)], last_x),
            (pltpu.roll(own, 1, 1), first_y),
            (pltpu.roll(own, 127, 1), last_y),
        )
        total = None
        inner = []
        for other, outside in others:
            w = face(own, jnp.where(outside, own, other))
            total = w if total is None else total + w
            inner.append(jnp.where(outside, 0.0, w))
        inverse = 1.0 / total
        at = pl.ds(row, CHUNK)
        diag[at] = total
        recip[at] = inverse
        for i, w in enumerate(inner):
            weights[i, at] = w * inverse

    def weight_chunk(z, q):
        row = start_row(z * per_plane + q)
        local = pl.ds(start_row(q), CHUNK)
        below = sig_halo[0, local] if z == 0 else sig[pl.ds(PAD + row - plane, CHUNK)]
        above = sig_halo[1, local] if z == depth - 1 else sig[pl.ds(PAD + row + plane, CHUNK)]
        first = (slab == 0) if z == 0 else False
        last = (slab == slabs - 1) if z == depth - 1 else False
        never = jnp.zeros((CHUNK, 128), jnp.int32)
        open_below = (never + first.astype(jnp.int32)) > 0 if z == 0 else never > 0
        open_above = (never + last.astype(jnp.int32)) > 0 if z == depth - 1 else never > 0
        make_weights(row, below, above, open_below, open_above)

    for z in [*range(1, depth - 1), 0, depth - 1]:
        if z == 0:
            for copy in sig_copies:
                copy.wait_recv()
        lax.fori_loop(0, per_plane, lambda q, _, z=z: (weight_chunk(z, q), 0)[1], 0)
    for copy in load_ints:
        copy.wait()

    def stage(k, c):
        def field(at):
            return x_in[c, at] if k == 0 else v[k - 1, c, at]

        cell = sources[c, group] - slab * (cells * 128) if k == 0 else None

        def work(row, below, above):
            here = pl.ds(PAD + row, plane)
            at = pl.ds(row, plane)
            mid = field(here)
            image = (
                weights[0, at] * below
                + weights[1, at] * above
                + weights[2, at] * field(pl.ds(PAD - 1 + row, plane))
                + weights[3, at] * field(pl.ds(PAD + 1 + row, plane))
                + weights[4, at] * pltpu.roll(mid, 1, 1)
                + weights[5, at] * pltpu.roll(mid, 127, 1)
            )
            if k == 0:
                ids = (
                    lax.broadcasted_iota(jnp.int32, (plane, 128), 0) + row
                ) * 128 + lax.broadcasted_iota(jnp.int32, (plane, 128), 1)
                new = jnp.where(ids == cell, recip[at], 0.0) + (image - mid)
            else:
                j = k - 1
                new = (1.0 / B[k]) * image + (-A[j] / B[k]) * mid
                if j:
                    new = new + (-B[j] / B[k]) * v[k - 2, c, here]
            v[k, c, here] = new

        def dots(q, sums):
            row = start_row(q)
            here = pl.ds(PAD + row, CHUNK)
            scaled = diag[pl.ds(row, CHUNK)] * v[k, c, here]
            out = []
            for i, total in enumerate(sums):
                product = scaled * v[i, c, here]
                for part in range(CHUNK // 8):
                    total = total + product[part * 8:(part + 1) * 8]
                out.append(total)
            return tuple(out)

        def inside(z, _):
            row = pl.multiple_of(z * plane, plane)
            work(row, field(pl.ds(PAD + row - plane, plane)), field(pl.ds(PAD + row + plane, plane)))
            return 0

        lax.fori_loop(1, depth - 1, inside, 0)
        sums = tuple(jnp.zeros((8, 128), jnp.float32) for _ in range(min(k + 1, ITERS)))
        sums = lax.fori_loop(per_plane, (depth - 1) * per_plane, dots, sums)

        from_left, from_right = halo_copies(k, c)
        to_right, to_left = halo_copies(k + 1, c) if k < ITERS else (None, None)
        from_left.wait_recv()
        work(0, halo[k, 0, c], field(pl.ds(PAD + plane, plane)))
        if to_left is not None:
            to_left.start()
        from_right.wait_recv()
        work(cells - plane, field(pl.ds(PAD + cells - 2 * plane, plane)), halo[k, 1, c])
        if to_right is not None:
            to_right.start()

        sums = lax.fori_loop(0, per_plane, dots, sums)
        sums = lax.fori_loop((depth - 1) * per_plane, depth * per_plane, dots, sums)
        for i, total in enumerate(sums):
            rows_acc[pl.ds(SLOT[i, k] * ncol + c, 1), :] = jnp.sum(total, axis=0, keepdims=True)

    for k in range(STAGES):
        def column(c, _, k=k):
            if k == 0:
                pltpu.make_async_copy(x_hbm.at[c], x_in.at[c, body], load_sem.at[1 + c]).wait()
            stage(k, c)
            return 0

        lax.fori_loop(0, ncol, column, 0)

    mine = jnp.sum(jnp.transpose(rows_acc[...]), axis=0, keepdims=True)
    x_parts[here_x] = mine
    x_copies = [
        remote(x_parts.at[here_x], x_parts.at[here_x], xs_send.at[d], xs_recv.at[d], at)
        for d, at in enumerate(x_peers)
    ]
    for copy in x_copies:
        copy.start()
    for copy in x_copies:
        copy.wait_recv()
    total = x_parts[0]
    for i in range(1, RING):
        total = total + x_parts[i]
    z_parts[here_z] = total
    z_copies = [
        remote(z_parts.at[here_z], z_parts.at[here_z], zs_send.at[d], zs_recv.at[d], at)
        for d, at in enumerate(z_peers)
    ]
    for copy in z_copies:
        copy.start()
    for copy in z_copies:
        copy.wait_recv()
    total = z_parts[0]
    for i in range(1, zs):
        total = total + z_parts[i]

    wide = jnp.broadcast_to(total, (8, 128))
    entries = {}
    for pair, at in SLOT.items():
        entries[pair] = wide if at == 0 else pltpu.roll(wide, 128 - at * ncol, 1)

    def gram(i, j):
        return entries[(i, j)] if i <= j and (i, j) in entries else entries[(j, i)]

    c_x, c_r = coefficients(gram)
    live = lax.broadcasted_iota(jnp.int32, (8, 128), 1) < counts[group]
    for j, value in enumerate(c_x + c_r):
        value = jnp.where(live, value, 0.0)
        for c in range(ncol):
            table[c, pl.ds(j, 1)] = jnp.broadcast_to(value[:1, c:c + 1], (1, 128))

    for copy in sig_copies + x_copies + z_copies:
        copy.wait_send()
    for k in range(STAGES):
        for c in range(ncol):
            for copy in halo_copies(k, c):
                copy.wait_send()


def combine_kernel(dims, x_in, v, diag, table, pot_hbm, res_hbm, pot, res, out_sem):
    ncol, cells = dims

    def out_copies(c):
        return (
            pltpu.make_async_copy(pot.at[c], pot_hbm.at[c], out_sem.at[0, c]),
            pltpu.make_async_copy(res.at[c], res_hbm.at[c], out_sem.at[1, c]),
        )

    for c in range(ncol):
        def combine(q, _, c=c):
            row = pl.multiple_of(q * CHUNK, CHUNK)
            here, at = pl.ds(PAD + row, CHUNK), pl.ds(row, CHUNK)
            new_x, new_r = x_in[c, here], None
            for j in range(STAGES):
                vec = v[j, c, here]
                if j < ITERS:
                    new_x = new_x + table[c, pl.ds(j, 1)] * vec
                term = table[c, pl.ds(ITERS + j, 1)] * vec
                new_r = term if new_r is None else new_r + term
            pot[c, at] = new_x
            res[c, at] = diag[at] * new_r
            return 0

        lax.fori_loop(0, cells // CHUNK, combine, 0)
        for copy in out_copies(c):
            copy.start()
    for c in range(ncol):
        for copy in out_copies(c):
            copy.wait()


def solution(mesh):
    slabs = mesh.shape["slab"]

    def shards(sigma, iterate, counts, sources):
        depth, rows, lanes = sigma.shape
        ncol = iterate.shape[0]
        cells = depth * rows
        zs = slabs // RING
        f32 = jnp.float32
        vmem = pltpu.VMEM
        dma = pltpu.SemaphoreType.DMA
        anywhere = pl.BlockSpec(memory_space=pl.ANY)
        on_chip = pl.BlockSpec(memory_space=pltpu.VMEM)

        def in_hbm(array):
            return pltpu.with_memory_space_constraint(array, pltpu.HBM)

        sources = sources.T
        held = pl.pallas_call(
            functools.partial(basis_kernel, (slabs, ncol, depth, rows)),
            out_shape=(
                vmem((ncol, cells + 2 * PAD, lanes), f32),
                vmem((STAGES, ncol, cells + 2 * PAD, lanes), f32),
                vmem((cells, lanes), f32),
                vmem((ncol, 16, lanes), f32),
            ),
            in_specs=[anywhere] * 4,
            out_specs=(on_chip,) * 4,
            scratch_shapes=[
                pltpu.SMEM(counts.shape, jnp.int32),
                pltpu.SMEM(sources.shape, jnp.int32),
                vmem((cells + 2 * PAD, lanes), f32),
                vmem((STAGES, 2, ncol, rows, lanes), f32),
                vmem((2, rows, lanes), f32),
                vmem((6, cells, lanes), f32),
                vmem((cells, lanes), f32),
                vmem((128, 128), f32),
                vmem((RING, 1, 128), f32),
                vmem((zs, 1, 128), f32),
                dma((3 + ncol,)),
                dma((2,)),
                dma((2,)),
                dma((STAGES, 2, ncol)),
                dma((STAGES, 2, ncol)),
                dma((RING - 1,)),
                dma((RING - 1,)),
                dma((zs - 1,)),
                dma((zs - 1,)),
            ],
            compiler_params=pltpu.CompilerParams(
                collective_id=0, has_side_effects=True, vmem_limit_bytes=24 * 1024 * 1024
            ),
        )(
            in_hbm(counts),
            in_hbm(sources),
            in_hbm(sigma.reshape(cells, lanes)),
            in_hbm(iterate.reshape(ncol, cells, lanes)),
        )
        flat = pltpu.HBM((ncol, cells, lanes), f32)
        potential, residual = pl.pallas_call(
            functools.partial(combine_kernel, (ncol, cells)),
            out_shape=(flat, flat),
            in_specs=[on_chip] * 4,
            out_specs=(anywhere, anywhere),
            scratch_shapes=[vmem((ncol, cells, lanes), f32), vmem((ncol, cells, lanes), f32), dma((2, ncol))],
            compiler_params=pltpu.CompilerParams(vmem_limit_bytes=24 * 1024 * 1024),
        )(*held)
        return potential.reshape(iterate.shape), residual.reshape(iterate.shape)

    return jax.shard_map(
        shards,
        mesh=mesh,
        in_specs=(P("slab", None, None), P("src", "slab", None, None), P(), P()),
        out_specs=(P("src", "slab", None, None), P("src", "slab", None, None)),
        check_vma=False,
    )
```

```python
import functools

import jax
import jax.numpy as jnp
from jax import lax
from jax.experimental import pallas as pl
from jax.experimental.pallas import tpu as pltpu
from jax.sharding import PartitionSpec as P

MESH = pl.DeviceIdType.MESH
ITERS = 6
STAGES = ITERS + 1
CORES = 2
PAD = 8
CHUNK = 64

A = (-0.1666, -0.13, -0.07, -0.02, -0.02, -0.01)
B = (0.0, 0.373, 0.458, 0.484, 0.487, 0.493, 0.495)

PAIRS = [(i, j) for j in range(STAGES) for i in range(min(j + 1, ITERS))]
SLOT = {pair: at for at, pair in enumerate(PAIRS)}


def face(first, second):
    return 2.0 * first * second / (first + second)


def coefficients(gram):
    zero = jnp.zeros_like(gram(0, 0))
    one = zero + 1.0
    c_r, c_p = [one], [one]
    c_x = [zero] * ITERS
    r_dot = [gram(0, l) for l in range(STAGES)]
    rz = r_dot[0]
    for step in range(ITERS):
        c_q = [zero] * (step + 2)
        for i in range(step + 1):
            c_q[i] = c_q[i] + (1.0 - A[i]) * c_p[i]
            c_q[i + 1] = c_q[i + 1] - B[i + 1] * c_p[i]
            if i:
                c_q[i - 1] = c_q[i - 1] - B[i] * c_p[i]
        q_dot = {
            l: functools.reduce(lambda s, t: s + t, [c_q[i] * gram(i, l) for i in range(step + 2)])
            for l in range(step, ITERS)
        }
        alpha = rz / (c_r[step] * q_dot[step])
        c_x = [c_x[i] + alpha * c_p[i] if i <= step else c_x[i] for i in range(ITERS)]
        c_r = [(c_r[i] if i <= step else zero) - alpha * c_q[i] for i in range(step + 2)]
        if step + 1 < ITERS:
            r_dot = {l: r_dot[l] - alpha * q_dot[l] for l in range(step + 1, ITERS)}
            rz_new = c_r[step + 1] * r_dot[step + 1]
            beta = rz_new / rz
            rz = rz_new
            c_p = [c_r[i] + (beta * c_p[i] if i <= step else zero) for i in range(step + 2)]
    return c_x, c_r


def basis_kernel(
    dims,
    counts_hbm, sources_hbm, sigma_hbm, x_hbm, x_in, v, diag, table,
    counts, sources, sig, halo, sig_halo, weights, recip, rows_acc, parts,
    load_sem, sig_send, sig_recv, send_sem, recv_sem, part_send, part_recv,
):
    slabs, ncol, depth, rows = dims
    cells = depth * rows
    plane = rows
    slab = lax.axis_index("slab")
    group = lax.axis_index("src")
    core = group % CORES
    twin = group - core + (CORES - 1 - core)
    left, right = (slab + slabs - 1) % slabs, (slab + 1) % slabs

    others = [(slab + d) % slabs for d in range(1, slabs)]
    body = pl.ds(PAD, cells)

    barrier = pltpu.get_barrier_semaphore()
    greeted = [(at, group) for at in others] + [(slab, twin)]
    for at in greeted:
        pl.semaphore_signal(barrier, inc=1, device_id=at, device_id_type=MESH)

    load_sig = pltpu.make_async_copy(sigma_hbm, sig.at[body], load_sem.at[0])
    load_sig.start()
    load_x = [pltpu.make_async_copy(x_hbm.at[c], x_in.at[c, body], load_sem.at[1 + c]) for c in range(ncol)]
    for copy in load_x:
        copy.start()
    load_ints = [
        pltpu.make_async_copy(counts_hbm, counts, load_sem.at[1 + ncol]),
        pltpu.make_async_copy(sources_hbm, sources, load_sem.at[2 + ncol]),
    ]
    for copy in load_ints:
        copy.start()

    pl.semaphore_wait(barrier, len(greeted))

    low_rows, high_rows = pl.ds(0, plane), pl.ds(cells - plane, plane)

    def remote(src, dst, send, recv, at, of=group):
        return pltpu.make_async_remote_copy(
            src_ref=src, dst_ref=dst, send_sem=send, recv_sem=recv, device_id=(at, of), device_id_type=MESH
        )

    edge = pl.ds(pl.multiple_of((1 - core) * (cells - plane), plane), plane)
    sig_out = remote(
        sigma_hbm.at[edge], sig_halo.at[core], sig_send.at[0], sig_recv.at[0],
        (slab + (1 - 2 * core) + slabs) % slabs,
    )
    sig_out.start()
    sig_share = remote(sig_halo.at[core], sig_halo.at[core], sig_send.at[1], sig_recv.at[1], slab, twin)

    def halo_copies(k, c):
        if k == 0:
            high, low = x_hbm.at[c, high_rows], x_hbm.at[c, low_rows]
        else:
            high = v.at[k - 1, c, pl.ds(PAD + cells - plane, plane)]
            low = v.at[k - 1, c, pl.ds(PAD, plane)]
        return (
            remote(high, halo.at[k, 0, c], send_sem.at[k, 0, c], recv_sem.at[k, 0, c], right),
            remote(low, halo.at[k, 1, c], send_sem.at[k, 1, c], recv_sem.at[k, 1, c], left),
        )

    for c in range(ncol):
        for copy in halo_copies(0, c):
            copy.start()

    blank = jnp.zeros((PAD, 128), jnp.float32)
    for c in range(ncol):
        x_in[c, pl.ds(0, PAD)] = blank
        x_in[c, pl.ds(PAD + cells, PAD)] = blank
        for k in range(STAGES):
            v[k, c, pl.ds(0, PAD)] = blank
            v[k, c, pl.ds(PAD + cells, PAD)] = blank
    sig[pl.ds(0, PAD)] = blank + 1.0
    sig[pl.ds(PAD + cells, PAD)] = blank + 1.0
    rows_acc[...] = jnp.zeros_like(rows_acc)

    load_sig.wait()

    lane = lax.broadcasted_iota(jnp.int32, (CHUNK, 128), 1)
    sub = lax.broadcasted_iota(jnp.int32, (CHUNK, 128), 0)
    per_plane = plane // CHUNK

    def start_row(q):
        return pl.multiple_of(q * CHUNK, CHUNK)

    def make_weights(row, below, above, open_below, open_above):
        own = sig[pl.ds(PAD + row, CHUNK)]
        x_at = sub + row % plane
        first_x, last_x = x_at == 0, x_at == plane - 1
        first_y, last_y = lane == 0, lane == 127
        others = (
            (below, open_below),
            (above, open_above),
            (sig[pl.ds(PAD - 1 + row, CHUNK)], first_x),
            (sig[pl.ds(PAD + 1 + row, CHUNK)], last_x),
            (pltpu.roll(own, 1, 1), first_y),
            (pltpu.roll(own, 127, 1), last_y),
        )
        total = None
        inner = []
        for other, outside in others:
            w = face(own, jnp.where(outside, own, other))
            total = w if total is None else total + w
            inner.append(jnp.where(outside, 0.0, w))
        inverse = 1.0 / total
        at = pl.ds(row, CHUNK)
        diag[at] = total
        recip[at] = inverse
        for i, w in enumerate(inner):
            weights[i, at] = w * inverse

    def weight_chunk(z, q):
        row = start_row(z * per_plane + q)
        local = pl.ds(start_row(q), CHUNK)
        below = sig_halo[0, local] if z == 0 else sig[pl.ds(PAD + row - plane, CHUNK)]
        above = sig_halo[1, local] if z == depth - 1 else sig[pl.ds(PAD + row + plane, CHUNK)]
        first = (slab == 0) if z == 0 else False
        last = (slab == slabs - 1) if z == depth - 1 else False
        never = jnp.zeros((CHUNK, 128), jnp.int32)
        open_below = (never + first.astype(jnp.int32)) > 0 if z == 0 else never > 0
        open_above = (never + last.astype(jnp.int32)) > 0 if z == depth - 1 else never > 0
        make_weights(row, below, above, open_below, open_above)

    for z in [*range(1, depth - 1), 0, depth - 1]:
        if z == 0:
            sig_out.wait_recv()
            sig_share.start()
            sig_share.wait_recv()
        lax.fori_loop(0, per_plane, lambda q, _, z=z: (weight_chunk(z, q), 0)[1], 0)
    for copy in load_ints:
        copy.wait()

    def stage(k, c):
        def field(at):
            return x_in[c, at] if k == 0 else v[k - 1, c, at]

        cell = sources[c, group] - slab * (cells * 128) if k == 0 else None

        def work(row, below, above):
            here = pl.ds(PAD + row, plane)
            at = pl.ds(row, plane)
            mid = field(here)
            image = (
                weights[0, at] * below
                + weights[1, at] * above
                + weights[2, at] * field(pl.ds(PAD - 1 + row, plane))
                + weights[3, at] * field(pl.ds(PAD + 1 + row, plane))
                + weights[4, at] * pltpu.roll(mid, 1, 1)
                + weights[5, at] * pltpu.roll(mid, 127, 1)
            )
            if k == 0:
                ids = (
                    lax.broadcasted_iota(jnp.int32, (plane, 128), 0) + row
                ) * 128 + lax.broadcasted_iota(jnp.int32, (plane, 128), 1)
                new = jnp.where(ids == cell, recip[at], 0.0) + (image - mid)
            else:
                j = k - 1
                new = (1.0 / B[k]) * image + (-A[j] / B[k]) * mid
                if j:
                    new = new + (-B[j] / B[k]) * v[k - 2, c, here]
            v[k, c, here] = new

        def dots(q, sums):
            row = start_row(q)
            here = pl.ds(PAD + row, CHUNK)
            scaled = diag[pl.ds(row, CHUNK)] * v[k, c, here]
            out = []
            for i, total in enumerate(sums):
                product = scaled * v[i, c, here]
                for part in range(CHUNK // 8):
                    total = total + product[part * 8:(part + 1) * 8]
                out.append(total)
            return tuple(out)

        def inside(z, _):
            row = pl.multiple_of(z * plane, plane)
            work(row, field(pl.ds(PAD + row - plane, plane)), field(pl.ds(PAD + row + plane, plane)))
            return 0

        lax.fori_loop(1, depth - 1, inside, 0)
        sums = tuple(jnp.zeros((8, 128), jnp.float32) for _ in range(min(k + 1, ITERS)))
        sums = lax.fori_loop(per_plane, (depth - 1) * per_plane, dots, sums)

        from_left, from_right = halo_copies(k, c)
        to_right, to_left = halo_copies(k + 1, c) if k < ITERS else (None, None)
        from_left.wait_recv()
        work(0, halo[k, 0, c], field(pl.ds(PAD + plane, plane)))
        if to_left is not None:
            to_left.start()
        from_right.wait_recv()
        work(cells - plane, field(pl.ds(PAD + cells - 2 * plane, plane)), halo[k, 1, c])
        if to_right is not None:
            to_right.start()

        sums = lax.fori_loop(0, per_plane, dots, sums)
        sums = lax.fori_loop((depth - 1) * per_plane, depth * per_plane, dots, sums)
        for i, total in enumerate(sums):
            rows_acc[pl.ds(SLOT[i, k] * ncol + c, 1), :] = jnp.sum(total, axis=0, keepdims=True)

    for k in range(STAGES):
        def column(c, _, k=k):
            if k == 0:
                pltpu.make_async_copy(x_hbm.at[c], x_in.at[c, body], load_sem.at[1 + c]).wait()
            stage(k, c)
            return 0

        lax.fori_loop(0, ncol, column, 0)

    mine = jnp.sum(jnp.transpose(rows_acc[...]), axis=0, keepdims=True)
    parts[slab] = mine
    part_copies = [remote(parts.at[slab], parts.at[slab], part_send, part_recv, at) for at in others]
    for copy in part_copies:
        copy.start()
    sig_out.wait_send()
    sig_share.wait_send()
    for k in range(STAGES):
        def sent(c, _, k=k):
            for copy in halo_copies(k, c):
                copy.wait_send()
            return 0

        lax.fori_loop(0, ncol, sent, 0)
    every = parts.at[pl.ds(0, slabs - 1)]
    all_parts = remote(every, every, part_send, part_recv, right)
    all_parts.wait_recv()
    terms = [parts[i] for i in range(slabs)]
    while len(terms) > 1:
        terms = [sum(terms[i:i + 2][1:], terms[i]) for i in range(0, len(terms), 2)]
    total = terms[0]

    wide = jnp.broadcast_to(total, (8, 128))
    entries = {}
    for pair, at in SLOT.items():
        entries[pair] = wide if at == 0 else pltpu.roll(wide, 128 - at * ncol, 1)

    def gram(i, j):
        return entries[(i, j)] if i <= j and (i, j) in entries else entries[(j, i)]

    c_x, c_r = coefficients(gram)
    live = lax.broadcasted_iota(jnp.int32, (8, 128), 1) < counts[group]
    for j, value in enumerate(c_x + c_r):
        value = jnp.where(live, value, 0.0)
        for c in range(ncol):
            table[c, pl.ds(j, 1)] = jnp.broadcast_to(value[:1, c:c + 1], (1, 128))

    all_parts.wait_send()


def combine_kernel(dims, x_in, v, diag, table, pot_hbm, res_hbm, pot, res, out_sem):
    ncol, cells, plane = dims

    def out_copies(c, row):
        at = pl.ds(row, plane)
        return (
            pltpu.make_async_copy(pot.at[c, at], pot_hbm.at[c, at], out_sem.at[0, c, row // plane]),
            pltpu.make_async_copy(res.at[c, at], res_hbm.at[c, at], out_sem.at[1, c, row // plane]),
        )

    for c in range(ncol):
        def combine(z, _, c=c):
            row = pl.multiple_of(z * plane, plane)
            here, at = pl.ds(PAD + row, plane), pl.ds(row, plane)
            new_x, new_r = x_in[c, here], None
            for j in range(STAGES):
                vec = v[j, c, here]
                if j < ITERS:
                    new_x = new_x + table[c, pl.ds(j, 1)] * vec
                term = table[c, pl.ds(ITERS + j, 1)] * vec
                new_r = term if new_r is None else new_r + term
            pot[c, at] = new_x
            res[c, at] = diag[at] * new_r
            for copy in out_copies(c, row):
                copy.start()
            return 0

        lax.fori_loop(0, cells // plane, combine, 0)
    for c in range(ncol):
        for row in range(0, cells, plane):
            for copy in out_copies(c, row):
                copy.wait()


def solution(mesh):
    slabs = mesh.shape["slab"]

    def shards(sigma, iterate, counts, sources):
        depth, rows, lanes = sigma.shape
        ncol = iterate.shape[0]
        cells = depth * rows
        f32 = jnp.float32
        vmem = pltpu.VMEM
        dma = pltpu.SemaphoreType.DMA
        anywhere = pl.BlockSpec(memory_space=pl.ANY)
        on_chip = pl.BlockSpec(memory_space=pltpu.VMEM)

        def in_hbm(array):
            return pltpu.with_memory_space_constraint(array, pltpu.HBM)

        sources = sources.T
        held = pl.pallas_call(
            functools.partial(basis_kernel, (slabs, ncol, depth, rows)),
            out_shape=(
                vmem((ncol, cells + 2 * PAD, lanes), f32),
                vmem((STAGES, ncol, cells + 2 * PAD, lanes), f32),
                vmem((cells, lanes), f32),
                vmem((ncol, 16, lanes), f32),
            ),
            in_specs=[anywhere] * 4,
            out_specs=(on_chip,) * 4,
            scratch_shapes=[
                pltpu.SMEM(counts.shape, jnp.int32),
                pltpu.SMEM(sources.shape, jnp.int32),
                vmem((cells + 2 * PAD, lanes), f32),
                vmem((STAGES, 2, ncol, rows, lanes), f32),
                vmem((2, rows, lanes), f32),
                vmem((6, cells, lanes), f32),
                vmem((cells, lanes), f32),
                vmem((128, 128), f32),
                vmem((slabs, 1, 128), f32),
                dma((3 + ncol,)),
                dma((2,)),
                dma((2,)),
                dma((STAGES, 2, ncol)),
                dma((STAGES, 2, ncol)),
                dma,
                dma,
            ],
            compiler_params=pltpu.CompilerParams(
                collective_id=0, has_side_effects=True, vmem_limit_bytes=24 * 1024 * 1024
            ),
        )(
            in_hbm(counts),
            in_hbm(sources),
            in_hbm(sigma.reshape(cells, lanes)),
            in_hbm(iterate.reshape(ncol, cells, lanes)),
        )
        flat = pltpu.HBM((ncol, cells, lanes), f32)
        potential, residual = pl.pallas_call(
            functools.partial(combine_kernel, (ncol, cells, rows)),
            out_shape=(flat, flat),
            in_specs=[on_chip] * 4,
            out_specs=(anywhere, anywhere),
            scratch_shapes=[vmem((ncol, cells, lanes), f32), vmem((ncol, cells, lanes), f32), dma((2, ncol, depth))],
            compiler_params=pltpu.CompilerParams(vmem_limit_bytes=24 * 1024 * 1024),
        )(*held)
        return potential.reshape(iterate.shape), residual.reshape(iterate.shape)

    return jax.shard_map(
        shards,
        mesh=mesh,
        in_specs=(P("slab", None, None), P("src", "slab", None, None), P(), P()),
        out_specs=(P("src", "slab", None, None), P("src", "slab", None, None)),
        check_vma=False,
    )
```

```python
import functools

import jax
import jax.numpy as jnp
from jax import lax
from jax.experimental import pallas as pl
from jax.experimental.pallas import tpu as pltpu
from jax.sharding import PartitionSpec as P

MESH = pl.DeviceIdType.MESH
ITERS = 6
STAGES = ITERS + 1
RING = 4
CORES = 2
PAD = 8
CHUNK = 64

A = (-0.1666, -0.13, -0.07, -0.02, -0.02, -0.01)
B = (0.0, 0.373, 0.458, 0.484, 0.487, 0.493, 0.495)

PAIRS = [(i, j) for j in range(ITERS) for i in range(j + 1)] + [(ITERS - 1, ITERS)]
SLOT = {pair: at for at, pair in enumerate(PAIRS)}


def face(first, second):
    return 2.0 * first * second / (first + second)


def coefficients(gram):
    zero = jnp.zeros_like(gram(0, 0))
    one = zero + 1.0
    c_r, c_p = [one], [one]
    c_x = [zero] * ITERS
    r_dot = [gram(0, l) for l in range(ITERS)]
    rz = r_dot[0]
    for step in range(ITERS):
        c_q = [zero] * (step + 2)
        for i in range(step + 1):
            c_q[i] = c_q[i] + (1.0 - A[i]) * c_p[i]
            c_q[i + 1] = c_q[i + 1] - B[i + 1] * c_p[i]
            if i:
                c_q[i - 1] = c_q[i - 1] - B[i] * c_p[i]
        q_dot = {
            l: functools.reduce(lambda s, t: s + t, [c_q[i] * gram(i, l) for i in range(step + 2)])
            for l in range(step, ITERS)
        }
        alpha = rz / (c_r[step] * q_dot[step])
        c_x = [c_x[i] + alpha * c_p[i] if i <= step else c_x[i] for i in range(ITERS)]
        c_r = [(c_r[i] if i <= step else zero) - alpha * c_q[i] for i in range(step + 2)]
        if step + 1 < ITERS:
            r_dot = {l: r_dot[l] - alpha * q_dot[l] for l in range(step + 1, ITERS)}
            rz_new = c_r[step + 1] * r_dot[step + 1]
            beta = rz_new / rz
            rz = rz_new
            c_p = [c_r[i] + (beta * c_p[i] if i <= step else zero) for i in range(step + 2)]
    return c_x, c_r


def basis_kernel(
    dims,
    counts_hbm, sources_hbm, sigma_hbm, x_hbm, x_in, v, diag, table,
    counts, sources, sig, halo, sig_halo, weights, recip, rows_acc, last_acc, parts,
    load_sem, sig_send, sig_recv, send_sem, recv_sem, part_send, part_recv,
):
    slabs, ncol, depth, rows = dims
    cells = depth * rows
    plane = rows
    slab = lax.axis_index("slab")
    group = lax.axis_index("src")
    core = group % CORES
    twin = group - core + (CORES - 1 - core)
    left, right = (slab + slabs - 1) % slabs, (slab + 1) % slabs

    deep = slabs // RING
    here_z, here_x = slab // RING, slab % RING
    steps = [(dz, dx) for dz in range(deep) for dx in range(RING) if dz or dx]
    steps.sort(key=lambda step: -min(step[0], deep - step[0]) - min(step[1], RING - step[1]))
    others = [((here_z + dz) % deep) * RING + (here_x + dx) % RING for dz, dx in steps]
    body = pl.ds(PAD, cells)

    barrier = pltpu.get_barrier_semaphore()
    greeted = [(at, group) for at in others] + [(slab, twin)]
    for at in greeted:
        pl.semaphore_signal(barrier, inc=1, device_id=at, device_id_type=MESH)

    load_sig = pltpu.make_async_copy(sigma_hbm, sig.at[body], load_sem.at[0])
    load_sig.start()
    load_x = [pltpu.make_async_copy(x_hbm.at[c], x_in.at[c, body], load_sem.at[1 + c]) for c in range(ncol)]
    for copy in load_x:
        copy.start()
    load_ints = [
        pltpu.make_async_copy(counts_hbm, counts, load_sem.at[1 + ncol]),
        pltpu.make_async_copy(sources_hbm, sources, load_sem.at[2 + ncol]),
    ]
    for copy in load_ints:
        copy.start()

    pl.semaphore_wait(barrier, len(greeted))

    low_rows, high_rows = pl.ds(0, plane), pl.ds(cells - plane, plane)

    def remote(src, dst, send, recv, at, of=group):
        return pltpu.make_async_remote_copy(
            src_ref=src, dst_ref=dst, send_sem=send, recv_sem=recv, device_id=(at, of), device_id_type=MESH
        )

    edge = pl.ds(pl.multiple_of((1 - core) * (cells - plane), plane), plane)
    sig_out = remote(
        sigma_hbm.at[edge], sig_halo.at[core], sig_send.at[0], sig_recv.at[0],
        (slab + (1 - 2 * core) + slabs) % slabs,
    )
    sig_out.start()
    sig_share = remote(sig_halo.at[core], sig_halo.at[core], sig_send.at[1], sig_recv.at[1], slab, twin)

    def halo_copies(k, c):
        if k == 0:
            high, low = x_hbm.at[c, high_rows], x_hbm.at[c, low_rows]
        else:
            high = v.at[k - 1, c, pl.ds(PAD + cells - plane, plane)]
            low = v.at[k - 1, c, pl.ds(PAD, plane)]
        return (
            remote(high, halo.at[k, 0, c], send_sem.at[k, 0, c], recv_sem.at[k, 0, c], right),
            remote(low, halo.at[k, 1, c], send_sem.at[k, 1, c], recv_sem.at[k, 1, c], left),
        )

    for c in range(ncol):
        for copy in halo_copies(0, c):
            copy.start()

    blank = jnp.zeros((PAD, 128), jnp.float32)
    for c in range(ncol):
        x_in[c, pl.ds(0, PAD)] = blank
        x_in[c, pl.ds(PAD + cells, PAD)] = blank
        for k in range(STAGES):
            v[k, c, pl.ds(0, PAD)] = blank
            v[k, c, pl.ds(PAD + cells, PAD)] = blank
    sig[pl.ds(0, PAD)] = blank + 1.0
    sig[pl.ds(PAD + cells, PAD)] = blank + 1.0
    rows_acc[...] = jnp.zeros_like(rows_acc)
    last_acc[...] = jnp.zeros_like(last_acc)

    load_sig.wait()

    lane = lax.broadcasted_iota(jnp.int32, (CHUNK, 128), 1)
    sub = lax.broadcasted_iota(jnp.int32, (CHUNK, 128), 0)
    per_plane = plane // CHUNK

    def start_row(q):
        return pl.multiple_of(q * CHUNK, CHUNK)

    def set_weights(at, total, inner):
        inverse = 1.0 / total
        diag[at] = total
        recip[at] = inverse
        for i, w in enumerate(inner):
            weights[i, at] = w * inverse

    def weight_chunk(z, q):
        row = start_row(z * per_plane + q)
        at = pl.ds(row, CHUNK)
        own = sig[pl.ds(PAD + row, CHUNK)]
        x_at = sub + row % plane
        first_x, last_x = x_at == 0, x_at == plane - 1
        first_y, last_y = lane == 0, lane == 127
        others = [
            None if z == 0 else (sig[pl.ds(PAD + row - plane, CHUNK)], None),
            None if z == depth - 1 else (sig[pl.ds(PAD + row + plane, CHUNK)], None),
            (sig[pl.ds(PAD - 1 + row, CHUNK)], first_x),
            (sig[pl.ds(PAD + 1 + row, CHUNK)], last_x),
            (pltpu.roll(own, 1, 1), first_y),
            (pltpu.roll(own, 127, 1), last_y),
        ]
        total = None
        inner = {}
        for i, pair in enumerate(others):
            if pair is None:
                continue
            other, outside = pair
            w = face(own, other if outside is None else jnp.where(outside, own, other))
            total = w if total is None else total + w
            inner[i] = w if outside is None else jnp.where(outside, 0.0, w)
        if 0 < z < depth - 1:
            set_weights(at, total, [inner[i] for i in range(6)])
        else:
            diag[at] = total
            for i, w in inner.items():
                weights[i, at] = w

    def finish_chunk(z, q):
        side = 0 if z == 0 else 1
        row = start_row(z * per_plane + q)
        at = pl.ds(row, CHUNK)
        own = sig[pl.ds(PAD + row, CHUNK)]
        end = (slab == (0 if side == 0 else slabs - 1)).astype(jnp.int32)
        outside = (jnp.zeros((CHUNK, 128), jnp.int32) + end) > 0
        w = face(own, jnp.where(outside, own, sig_halo[side, pl.ds(start_row(q), CHUNK)]))
        inner = [weights[i, at] for i in range(6) if i != side]
        inner.insert(side, jnp.where(outside, 0.0, w))
        set_weights(at, diag[at] + w, inner)

    for z in [0, depth - 1, *range(1, depth - 1)]:
        lax.fori_loop(0, per_plane, lambda q, _, z=z: (weight_chunk(z, q), 0)[1], 0)
    sig_out.wait_recv()
    sig_share.start()
    sig_share.wait_recv()
    for z in (0, depth - 1):
        lax.fori_loop(0, per_plane, lambda q, _, z=z: (finish_chunk(z, q), 0)[1], 0)
    for copy in load_ints:
        copy.wait()

    def stage(k, c):
        def field(at):
            return x_in[c, at] if k == 0 else v[k - 1, c, at]

        firsts = range(k + 1) if k < ITERS else (ITERS - 1,)
        cell = sources[c, group] - slab * (cells * 128) if k == 0 else None

        def work(row, below, above):
            here = pl.ds(PAD + row, plane)
            at = pl.ds(row, plane)
            mid = field(here)
            image = (
                weights[0, at] * below
                + weights[1, at] * above
                + weights[2, at] * field(pl.ds(PAD - 1 + row, plane))
                + weights[3, at] * field(pl.ds(PAD + 1 + row, plane))
                + weights[4, at] * pltpu.roll(mid, 1, 1)
                + weights[5, at] * pltpu.roll(mid, 127, 1)
            )
            if k == 0:
                ids = (
                    lax.broadcasted_iota(jnp.int32, (plane, 128), 0) + row
                ) * 128 + lax.broadcasted_iota(jnp.int32, (plane, 128), 1)
                new = jnp.where(ids == cell, recip[at], 0.0) + (image - mid)
            else:
                j = k - 1
                new = (1.0 / B[k]) * image + (-A[j] / B[k]) * mid
                if j:
                    new = new + (-B[j] / B[k]) * v[k - 2, c, here]
            v[k, c, here] = new

        def dots(q, sums):
            row = start_row(q)
            here = pl.ds(PAD + row, CHUNK)
            scaled = diag[pl.ds(row, CHUNK)] * v[k, c, here]
            out = []
            for i, total in zip(firsts, sums):
                product = scaled * v[i, c, here]
                for part in range(CHUNK // 8):
                    total = total + product[part * 8:(part + 1) * 8]
                out.append(total)
            return tuple(out)

        def inside(z, _):
            row = pl.multiple_of(z * plane, plane)
            work(row, field(pl.ds(PAD + row - plane, plane)), field(pl.ds(PAD + row + plane, plane)))
            return 0

        lax.fori_loop(1, depth - 1, inside, 0)
        sums = tuple(jnp.zeros((8, 128), jnp.float32) for _ in firsts)
        sums = lax.fori_loop(per_plane, (depth - 1) * per_plane, dots, sums)

        from_left, from_right = halo_copies(k, c)
        to_right, to_left = halo_copies(k + 1, c) if k < ITERS else (None, None)
        from_left.wait_recv()
        work(0, halo[k, 0, c], field(pl.ds(PAD + plane, plane)))
        if to_left is not None:
            to_left.start()
        from_right.wait_recv()
        work(cells - plane, field(pl.ds(PAD + cells - 2 * plane, plane)), halo[k, 1, c])
        if to_right is not None:
            to_right.start()

        sums = lax.fori_loop(0, per_plane, dots, sums)
        sums = lax.fori_loop((depth - 1) * per_plane, depth * per_plane, dots, sums)
        for i, total in zip(firsts, sums):
            row = jnp.sum(total, axis=0, keepdims=True)
            if k < ITERS:
                rows_acc[pl.ds(SLOT[i, k] * ncol + c, 1), :] = row
            else:
                last_acc[pl.ds(c, 1), :] = row

    for k in range(STAGES):
        if k == ITERS:
            mine = jnp.sum(jnp.transpose(rows_acc[...]), axis=0, keepdims=True)

        def column(c, _, k=k):
            if k == 0:
                pltpu.make_async_copy(x_hbm.at[c], x_in.at[c, body], load_sem.at[1 + c]).wait()
            stage(k, c)
            return 0

        lax.fori_loop(0, ncol, column, 0)

    spot = SLOT[ITERS - 1, ITERS] * ncol + lax.broadcasted_iota(jnp.int32, (8, 128), 0)
    last = jnp.where(
        lax.broadcasted_iota(jnp.int32, (8, 128), 1) == spot, jnp.sum(last_acc[...], axis=1, keepdims=True), 0.0
    )
    parts[slab] = mine + jnp.sum(last, axis=0, keepdims=True)
    part_copies = [remote(parts.at[slab], parts.at[slab], part_send, part_recv, at) for at in others]
    for copy in part_copies:
        copy.start()
    sig_out.wait_send()
    sig_share.wait_send()
    for k in range(STAGES):
        def sent(c, _, k=k):
            for copy in halo_copies(k, c):
                copy.wait_send()
            return 0

        lax.fori_loop(0, ncol, sent, 0)
    every = parts.at[pl.ds(0, slabs - 1)]
    all_parts = remote(every, every, part_send, part_recv, right)
    all_parts.wait_recv()
    terms = [parts[i] for i in range(slabs)]
    while len(terms) > 1:
        terms = [sum(terms[i:i + 2][1:], terms[i]) for i in range(0, len(terms), 2)]
    total = terms[0]

    wide = jnp.broadcast_to(total, (8, 128))
    entries = {}
    for pair, at in SLOT.items():
        entries[pair] = wide if at == 0 else pltpu.roll(wide, 128 - at * ncol, 1)

    def gram(i, j):
        return entries[(i, j)] if i <= j and (i, j) in entries else entries[(j, i)]

    c_x, c_r = coefficients(gram)
    live = lax.broadcasted_iota(jnp.int32, (8, 128), 1) < counts[group]
    for j, value in enumerate(c_x + c_r):
        value = jnp.where(live, value, 0.0)
        for c in range(ncol):
            table[c, pl.ds(j, 1)] = jnp.broadcast_to(value[:1, c:c + 1], (1, 128))

    all_parts.wait_send()


def combine_kernel(dims, x_in, v, diag, table, pot_hbm, res_hbm, pot, res, out_sem):
    ncol, cells, plane = dims

    def out_copies(c, row):
        at = pl.ds(row, plane)
        return (
            pltpu.make_async_copy(pot.at[c, at], pot_hbm.at[c, at], out_sem.at[0, c, row // plane]),
            pltpu.make_async_copy(res.at[c, at], res_hbm.at[c, at], out_sem.at[1, c, row // plane]),
        )

    for c in range(ncol):
        def combine(z, _, c=c):
            row = pl.multiple_of(z * plane, plane)
            here, at = pl.ds(PAD + row, plane), pl.ds(row, plane)
            new_x, new_r = x_in[c, here], None
            for j in range(STAGES):
                vec = v[j, c, here]
                if j < ITERS:
                    new_x = new_x + table[c, pl.ds(j, 1)] * vec
                term = table[c, pl.ds(ITERS + j, 1)] * vec
                new_r = term if new_r is None else new_r + term
            pot[c, at] = new_x
            res[c, at] = diag[at] * new_r
            for copy in out_copies(c, row):
                copy.start()
            return 0

        lax.fori_loop(0, cells // plane, combine, 0)
    for c in range(ncol):
        for row in range(0, cells, plane):
            for copy in out_copies(c, row):
                copy.wait()


def solution(mesh):
    slabs = mesh.shape["slab"]

    def shards(sigma, iterate, counts, sources):
        depth, rows, lanes = sigma.shape
        ncol = iterate.shape[0]
        cells = depth * rows
        f32 = jnp.float32
        vmem = pltpu.VMEM
        dma = pltpu.SemaphoreType.DMA
        anywhere = pl.BlockSpec(memory_space=pl.ANY)
        on_chip = pl.BlockSpec(memory_space=pltpu.VMEM)

        def in_hbm(array):
            return pltpu.with_memory_space_constraint(array, pltpu.HBM)

        sources = sources.T
        held = pl.pallas_call(
            functools.partial(basis_kernel, (slabs, ncol, depth, rows)),
            out_shape=(
                vmem((ncol, cells + 2 * PAD, lanes), f32),
                vmem((STAGES, ncol, cells + 2 * PAD, lanes), f32),
                vmem((cells, lanes), f32),
                vmem((ncol, 16, lanes), f32),
            ),
            in_specs=[anywhere] * 4,
            out_specs=(on_chip,) * 4,
            scratch_shapes=[
                pltpu.SMEM(counts.shape, jnp.int32),
                pltpu.SMEM(sources.shape, jnp.int32),
                vmem((cells + 2 * PAD, lanes), f32),
                vmem((STAGES, 2, ncol, rows, lanes), f32),
                vmem((2, rows, lanes), f32),
                vmem((6, cells, lanes), f32),
                vmem((cells, lanes), f32),
                vmem((128, 128), f32),
                vmem((8, 128), f32),
                vmem((slabs, 1, 128), f32),
                dma((3 + ncol,)),
                dma((2,)),
                dma((2,)),
                dma((STAGES, 2, ncol)),
                dma((STAGES, 2, ncol)),
                dma,
                dma,
            ],
            compiler_params=pltpu.CompilerParams(
                collective_id=0, has_side_effects=True, vmem_limit_bytes=24 * 1024 * 1024
            ),
        )(
            in_hbm(counts),
            in_hbm(sources),
            in_hbm(sigma.reshape(cells, lanes)),
            in_hbm(iterate.reshape(ncol, cells, lanes)),
        )
        flat = pltpu.HBM((ncol, cells, lanes), f32)
        potential, residual = pl.pallas_call(
            functools.partial(combine_kernel, (ncol, cells, rows)),
            out_shape=(flat, flat),
            in_specs=[on_chip] * 4,
            out_specs=(anywhere, anywhere),
            scratch_shapes=[vmem((ncol, cells, lanes), f32), vmem((ncol, cells, lanes), f32), dma((2, ncol, depth))],
            compiler_params=pltpu.CompilerParams(vmem_limit_bytes=24 * 1024 * 1024),
        )(*held)
        return potential.reshape(iterate.shape), residual.reshape(iterate.shape)

    return jax.shard_map(
        shards,
        mesh=mesh,
        in_specs=(P("slab", None, None), P("src", "slab", None, None), P(), P()),
        out_specs=(P("src", "slab", None, None), P("src", "slab", None, None)),
        check_vma=False,
    )
```

```python
import functools

import jax
import jax.numpy as jnp
from jax import lax
from jax.experimental import pallas as pl
from jax.experimental.pallas import tpu as pltpu
from jax.sharding import PartitionSpec as P

MESH = pl.DeviceIdType.MESH
ITERS = 6
STAGES = ITERS + 1
RING = 4
CORES = 2
PAD = 8
CHUNK = 64

A = (-0.1666, -0.13, -0.07, -0.02, -0.02, -0.01)
B = (0.0, 0.373, 0.458, 0.484, 0.487, 0.493, 0.495)

PAIRS = [(i, j) for j in range(ITERS) for i in range(j + 1)] + [(ITERS - 1, ITERS)]
SLOT = {pair: at for at, pair in enumerate(PAIRS)}


def face(first, second):
    return 2.0 * first * second / (first + second)


def coefficients(gram):
    zero = jnp.zeros_like(gram(0, 0))
    one = zero + 1.0
    c_r, c_p = [one], [one]
    c_x = [zero] * ITERS
    r_dot = [gram(0, l) for l in range(ITERS)]
    rz = r_dot[0]
    for step in range(ITERS):
        c_q = [zero] * (step + 2)
        for i in range(step + 1):
            c_q[i] = c_q[i] + (1.0 - A[i]) * c_p[i]
            c_q[i + 1] = c_q[i + 1] - B[i + 1] * c_p[i]
            if i:
                c_q[i - 1] = c_q[i - 1] - B[i] * c_p[i]
        q_dot = {
            l: functools.reduce(lambda s, t: s + t, [c_q[i] * gram(i, l) for i in range(step + 2)])
            for l in range(step, ITERS)
        }
        alpha = rz / (c_r[step] * q_dot[step])
        c_x = [c_x[i] + alpha * c_p[i] if i <= step else c_x[i] for i in range(ITERS)]
        c_r = [(c_r[i] if i <= step else zero) - alpha * c_q[i] for i in range(step + 2)]
        if step + 1 < ITERS:
            r_dot = {l: r_dot[l] - alpha * q_dot[l] for l in range(step + 1, ITERS)}
            rz_new = c_r[step + 1] * r_dot[step + 1]
            beta = rz_new / rz
            rz = rz_new
            c_p = [c_r[i] + (beta * c_p[i] if i <= step else zero) for i in range(step + 2)]
    return c_x, c_r


def basis_kernel(
    dims,
    counts_hbm, sources_hbm, sigma_hbm, x_hbm, x_in, v, diag, table,
    counts, sources, sig, halo, sig_halo, weights, recip, rows_acc, last_acc, parts,
    load_sem, sig_send, sig_recv, send_sem, recv_sem, part_send, part_recv, known_sem,
):
    slabs, ncol, depth, rows = dims
    cells = depth * rows
    plane = rows
    slab = lax.axis_index("slab")
    group = lax.axis_index("src")
    core = group % CORES
    twin = group - core + (CORES - 1 - core)
    left, right = (slab + slabs - 1) % slabs, (slab + 1) % slabs

    deep = slabs // RING
    here_z, here_x = slab // RING, slab % RING
    steps = [(dz, dx) for dz in range(deep) for dx in range(RING) if dz or dx]
    steps.sort(key=lambda step: -min(step[0], deep - step[0]) - min(step[1], RING - step[1]))
    others = [((here_z + dz) % deep) * RING + (here_x + dx) % RING for dz, dx in steps]
    body = pl.ds(PAD, cells)

    barrier = pltpu.get_barrier_semaphore()
    greeted = [(left, group), (right, group), (slab, twin)]
    for at in greeted:
        pl.semaphore_signal(barrier, inc=1, device_id=at, device_id_type=MESH)

    load_sig = pltpu.make_async_copy(sigma_hbm, sig.at[body], load_sem.at[0])
    load_sig.start()
    load_x = [pltpu.make_async_copy(x_hbm.at[c], x_in.at[c, body], load_sem.at[1 + c]) for c in range(ncol)]
    for copy in load_x:
        copy.start()
    load_ints = [
        pltpu.make_async_copy(counts_hbm, counts, load_sem.at[1 + ncol]),
        pltpu.make_async_copy(sources_hbm, sources, load_sem.at[2 + ncol]),
    ]
    for copy in load_ints:
        copy.start()

    pl.semaphore_wait(barrier, len(greeted))

    low_rows, high_rows = pl.ds(0, plane), pl.ds(cells - plane, plane)

    def remote(src, dst, send, recv, at, of=group):
        return pltpu.make_async_remote_copy(
            src_ref=src, dst_ref=dst, send_sem=send, recv_sem=recv, device_id=(at, of), device_id_type=MESH
        )

    edge = pl.ds(pl.multiple_of((1 - core) * (cells - plane), plane), plane)
    sig_out = remote(
        sigma_hbm.at[edge], sig_halo.at[core], sig_send.at[0], sig_recv.at[0],
        (slab + (1 - 2 * core) + slabs) % slabs,
    )
    sig_out.start()
    sig_share = remote(sig_halo.at[core], sig_halo.at[core], sig_send.at[1], sig_recv.at[1], slab, twin)

    def halo_copies(k, c):
        if k == 0:
            high, low = x_hbm.at[c, high_rows], x_hbm.at[c, low_rows]
        else:
            high = v.at[k - 1, c, pl.ds(PAD + cells - plane, plane)]
            low = v.at[k - 1, c, pl.ds(PAD, plane)]
        return (
            remote(high, halo.at[k, 0, c], send_sem.at[k, 0, c], recv_sem.at[k, 0, c], right),
            remote(low, halo.at[k, 1, c], send_sem.at[k, 1, c], recv_sem.at[k, 1, c], left),
        )

    for c in range(ncol):
        for copy in halo_copies(0, c):
            copy.start()

    blank = jnp.zeros((PAD, 128), jnp.float32)
    for c in range(ncol):
        x_in[c, pl.ds(0, PAD)] = blank
        x_in[c, pl.ds(PAD + cells, PAD)] = blank
        for k in range(STAGES):
            v[k, c, pl.ds(0, PAD)] = blank
            v[k, c, pl.ds(PAD + cells, PAD)] = blank
    sig[pl.ds(0, PAD)] = blank + 1.0
    sig[pl.ds(PAD + cells, PAD)] = blank + 1.0
    rows_acc[...] = jnp.zeros_like(rows_acc)
    last_acc[...] = jnp.zeros_like(last_acc)

    load_sig.wait()

    lane = lax.broadcasted_iota(jnp.int32, (CHUNK, 128), 1)
    sub = lax.broadcasted_iota(jnp.int32, (CHUNK, 128), 0)
    per_plane = plane // CHUNK

    def start_row(q):
        return pl.multiple_of(q * CHUNK, CHUNK)

    def set_weights(at, total, inner):
        inverse = 1.0 / total
        diag[at] = total
        recip[at] = inverse
        for i, w in enumerate(inner):
            weights[i, at] = w * inverse

    def weight_chunk(z, q):
        row = start_row(z * per_plane + q)
        at = pl.ds(row, CHUNK)
        own = sig[pl.ds(PAD + row, CHUNK)]
        x_at = sub + row % plane
        first_x, last_x = x_at == 0, x_at == plane - 1
        first_y, last_y = lane == 0, lane == 127
        others = [
            None if z == 0 else (sig[pl.ds(PAD + row - plane, CHUNK)], None),
            None if z == depth - 1 else (sig[pl.ds(PAD + row + plane, CHUNK)], None),
            (sig[pl.ds(PAD - 1 + row, CHUNK)], first_x),
            (sig[pl.ds(PAD + 1 + row, CHUNK)], last_x),
            (pltpu.roll(own, 1, 1), first_y),
            (pltpu.roll(own, 127, 1), last_y),
        ]
        total = None
        inner = {}
        for i, pair in enumerate(others):
            if pair is None:
                continue
            other, outside = pair
            w = face(own, other if outside is None else jnp.where(outside, own, other))
            total = w if total is None else total + w
            inner[i] = w if outside is None else jnp.where(outside, 0.0, w)
        if 0 < z < depth - 1:
            set_weights(at, total, [inner[i] for i in range(6)])
        else:
            diag[at] = total
            for i, w in inner.items():
                weights[i, at] = w

    def finish_chunk(z, q):
        side = 0 if z == 0 else 1
        row = start_row(z * per_plane + q)
        at = pl.ds(row, CHUNK)
        own = sig[pl.ds(PAD + row, CHUNK)]
        end = (slab == (0 if side == 0 else slabs - 1)).astype(jnp.int32)
        outside = (jnp.zeros((CHUNK, 128), jnp.int32) + end) > 0
        w = face(own, jnp.where(outside, own, sig_halo[side, pl.ds(start_row(q), CHUNK)]))
        inner = [weights[i, at] for i in range(6) if i != side]
        inner.insert(side, jnp.where(outside, 0.0, w))
        set_weights(at, diag[at] + w, inner)

    for z in [0, depth - 1, *range(1, depth - 1)]:
        lax.fori_loop(0, per_plane, lambda q, _, z=z: (weight_chunk(z, q), 0)[1], 0)
    sig_out.wait_recv()
    sig_share.start()
    sig_share.wait_recv()
    for z in (0, depth - 1):
        lax.fori_loop(0, per_plane, lambda q, _, z=z: (finish_chunk(z, q), 0)[1], 0)
    for copy in load_ints:
        copy.wait()

    def stage(k, c):
        def field(at):
            return x_in[c, at] if k == 0 else v[k - 1, c, at]

        firsts = range(k + 1) if k < ITERS else (ITERS - 1,)
        cell = sources[c, group] - slab * (cells * 128) if k == 0 else None

        def work(row, below, above):
            here = pl.ds(PAD + row, plane)
            at = pl.ds(row, plane)
            mid = field(here)
            image = (
                weights[0, at] * below
                + weights[1, at] * above
                + weights[2, at] * field(pl.ds(PAD - 1 + row, plane))
                + weights[3, at] * field(pl.ds(PAD + 1 + row, plane))
                + weights[4, at] * pltpu.roll(mid, 1, 1)
                + weights[5, at] * pltpu.roll(mid, 127, 1)
            )
            if k == 0:
                ids = (
                    lax.broadcasted_iota(jnp.int32, (plane, 128), 0) + row
                ) * 128 + lax.broadcasted_iota(jnp.int32, (plane, 128), 1)
                new = jnp.where(ids == cell, recip[at], 0.0) + (image - mid)
            else:
                j = k - 1
                new = (1.0 / B[k]) * image + (-A[j] / B[k]) * mid
                if j:
                    new = new + (-B[j] / B[k]) * v[k - 2, c, here]
            v[k, c, here] = new

        def dots(q, sums):
            row = start_row(q)
            here = pl.ds(PAD + row, CHUNK)
            scaled = diag[pl.ds(row, CHUNK)] * v[k, c, here]
            out = []
            for i, total in zip(firsts, sums):
                product = scaled * v[i, c, here]
                for part in range(CHUNK // 8):
                    total = total + product[part * 8:(part + 1) * 8]
                out.append(total)
            return tuple(out)

        def inside(z, _):
            row = pl.multiple_of(z * plane, plane)
            work(row, field(pl.ds(PAD + row - plane, plane)), field(pl.ds(PAD + row + plane, plane)))
            return 0

        lax.fori_loop(1, depth - 1, inside, 0)
        sums = tuple(jnp.zeros((8, 128), jnp.float32) for _ in firsts)
        sums = lax.fori_loop(per_plane, (depth - 1) * per_plane, dots, sums)

        from_left, from_right = halo_copies(k, c)
        to_right, to_left = halo_copies(k + 1, c) if k < ITERS else (None, None)
        from_left.wait_recv()
        work(0, halo[k, 0, c], field(pl.ds(PAD + plane, plane)))
        if to_left is not None:
            to_left.start()
        from_right.wait_recv()
        work(cells - plane, field(pl.ds(PAD + cells - 2 * plane, plane)), halo[k, 1, c])
        if to_right is not None:
            to_right.start()

        sums = lax.fori_loop(0, per_plane, dots, sums)
        sums = lax.fori_loop((depth - 1) * per_plane, depth * per_plane, dots, sums)
        for i, total in zip(firsts, sums):
            row = jnp.sum(total, axis=0, keepdims=True)
            if k < ITERS:
                rows_acc[pl.ds(SLOT[i, k] * ncol + c, 1), :] = row
            else:
                last_acc[pl.ds(c, 1), :] = row

    reach = [4]
    while 2 * reach[-1] < slabs:
        reach.append(2 * reach[-1])
    rounds = reach[:-1]

    for k in range(STAGES):
        at_round = k - 4
        if 1 <= at_round <= len(rounds):
            for side in range(2):
                pl.semaphore_wait(known_sem.at[at_round - 1, side], 1)
        if 0 <= at_round < len(rounds):
            for side, far in enumerate((rounds[at_round], slabs - rounds[at_round])):
                pl.semaphore_signal(
                    known_sem.at[at_round, side], inc=1,
                    device_id=((slab + far) % slabs, group), device_id_type=MESH,
                )
        if k == ITERS:
            mine = jnp.sum(jnp.transpose(rows_acc[...]), axis=0, keepdims=True)

        def column(c, _, k=k):
            if k == 0:
                pltpu.make_async_copy(x_hbm.at[c], x_in.at[c, body], load_sem.at[1 + c]).wait()
            stage(k, c)
            return 0

        lax.fori_loop(0, ncol, column, 0)

    spot = SLOT[ITERS - 1, ITERS] * ncol + lax.broadcasted_iota(jnp.int32, (8, 128), 0)
    last = jnp.where(
        lax.broadcasted_iota(jnp.int32, (8, 128), 1) == spot, jnp.sum(last_acc[...], axis=1, keepdims=True), 0.0
    )
    parts[slab] = mine + jnp.sum(last, axis=0, keepdims=True)
    part_copies = [remote(parts.at[slab], parts.at[slab], part_send, part_recv, at) for at in others]
    for copy in part_copies:
        copy.start()
    sig_out.wait_send()
    sig_share.wait_send()
    for k in range(STAGES):
        def sent(c, _, k=k):
            for copy in halo_copies(k, c):
                copy.wait_send()
            return 0

        lax.fori_loop(0, ncol, sent, 0)
    every = parts.at[pl.ds(0, slabs - 1)]
    all_parts = remote(every, every, part_send, part_recv, right)
    all_parts.wait_recv()
    terms = [parts[i] for i in range(slabs)]
    while len(terms) > 1:
        terms = [sum(terms[i:i + 2][1:], terms[i]) for i in range(0, len(terms), 2)]
    total = terms[0]

    wide = jnp.broadcast_to(total, (8, 128))
    entries = {}
    for pair, at in SLOT.items():
        entries[pair] = wide if at == 0 else pltpu.roll(wide, 128 - at * ncol, 1)

    def gram(i, j):
        return entries[(i, j)] if i <= j and (i, j) in entries else entries[(j, i)]

    c_x, c_r = coefficients(gram)
    live = lax.broadcasted_iota(jnp.int32, (8, 128), 1) < counts[group]
    for j, value in enumerate(c_x + c_r):
        value = jnp.where(live, value, 0.0)
        for c in range(ncol):
            table[c, pl.ds(j, 1)] = jnp.broadcast_to(value[:1, c:c + 1], (1, 128))

    all_parts.wait_send()


def combine_kernel(dims, x_in, v, diag, table, pot_hbm, res_hbm, pot, res, out_sem):
    ncol, cells, plane = dims

    def out_copies(c, row):
        at = pl.ds(row, plane)
        return (
            pltpu.make_async_copy(pot.at[c, at], pot_hbm.at[c, at], out_sem.at[0, c, row // plane]),
            pltpu.make_async_copy(res.at[c, at], res_hbm.at[c, at], out_sem.at[1, c, row // plane]),
        )

    for c in range(ncol):
        def combine(z, _, c=c):
            row = pl.multiple_of(z * plane, plane)
            here, at = pl.ds(PAD + row, plane), pl.ds(row, plane)
            new_x, new_r = x_in[c, here], None
            for j in range(STAGES):
                vec = v[j, c, here]
                if j < ITERS:
                    new_x = new_x + table[c, pl.ds(j, 1)] * vec
                term = table[c, pl.ds(ITERS + j, 1)] * vec
                new_r = term if new_r is None else new_r + term
            pot[c, at] = new_x
            res[c, at] = diag[at] * new_r
            for copy in out_copies(c, row):
                copy.start()
            return 0

        lax.fori_loop(0, cells // plane, combine, 0)
    for c in range(ncol):
        for row in range(0, cells, plane):
            for copy in out_copies(c, row):
                copy.wait()


def solution(mesh):
    slabs = mesh.shape["slab"]

    def shards(sigma, iterate, counts, sources):
        depth, rows, lanes = sigma.shape
        ncol = iterate.shape[0]
        cells = depth * rows
        f32 = jnp.float32
        vmem = pltpu.VMEM
        dma = pltpu.SemaphoreType.DMA
        anywhere = pl.BlockSpec(memory_space=pl.ANY)
        on_chip = pl.BlockSpec(memory_space=pltpu.VMEM)

        def in_hbm(array):
            return pltpu.with_memory_space_constraint(array, pltpu.HBM)

        sources = sources.T
        held = pl.pallas_call(
            functools.partial(basis_kernel, (slabs, ncol, depth, rows)),
            out_shape=(
                vmem((ncol, cells + 2 * PAD, lanes), f32),
                vmem((STAGES, ncol, cells + 2 * PAD, lanes), f32),
                vmem((cells, lanes), f32),
                vmem((ncol, 16, lanes), f32),
            ),
            in_specs=[anywhere] * 4,
            out_specs=(on_chip,) * 4,
            scratch_shapes=[
                pltpu.SMEM(counts.shape, jnp.int32),
                pltpu.SMEM(sources.shape, jnp.int32),
                vmem((cells + 2 * PAD, lanes), f32),
                vmem((STAGES, 2, ncol, rows, lanes), f32),
                vmem((2, rows, lanes), f32),
                vmem((6, cells, lanes), f32),
                vmem((cells, lanes), f32),
                vmem((128, 128), f32),
                vmem((8, 128), f32),
                vmem((slabs, 1, 128), f32),
                dma((3 + ncol,)),
                dma((2,)),
                dma((2,)),
                dma((STAGES, 2, ncol)),
                dma((STAGES, 2, ncol)),
                dma,
                dma,
                pltpu.SemaphoreType.REGULAR((2, 2)),
            ],
            compiler_params=pltpu.CompilerParams(
                collective_id=0, has_side_effects=True, vmem_limit_bytes=24 * 1024 * 1024
            ),
        )(
            in_hbm(counts),
            in_hbm(sources),
            in_hbm(sigma.reshape(cells, lanes)),
            in_hbm(iterate.reshape(ncol, cells, lanes)),
        )
        flat = pltpu.HBM((ncol, cells, lanes), f32)
        potential, residual = pl.pallas_call(
            functools.partial(combine_kernel, (ncol, cells, rows)),
            out_shape=(flat, flat),
            in_specs=[on_chip] * 4,
            out_specs=(anywhere, anywhere),
            scratch_shapes=[vmem((ncol, cells, lanes), f32), vmem((ncol, cells, lanes), f32), dma((2, ncol, depth))],
            compiler_params=pltpu.CompilerParams(vmem_limit_bytes=24 * 1024 * 1024),
        )(*held)
        return potential.reshape(iterate.shape), residual.reshape(iterate.shape)

    return jax.shard_map(
        shards,
        mesh=mesh,
        in_specs=(P("slab", None, None), P("src", "slab", None, None), P(), P()),
        out_specs=(P("src", "slab", None, None), P("src", "slab", None, None)),
        check_vma=False,
    )
```

```python
import functools

import jax
import jax.numpy as jnp
from jax import lax
from jax.experimental import pallas as pl
from jax.experimental.pallas import tpu as pltpu
from jax.sharding import PartitionSpec as P

MESH = pl.DeviceIdType.MESH
ITERS = 6
STAGES = ITERS + 1
RING = 4
CORES = 2
PAD = 8
CHUNK = 64

A = (-0.1666, -0.13, -0.07, -0.02, -0.02, -0.01)
B = (0.0, 0.373, 0.458, 0.484, 0.487, 0.493, 0.495)

PAIRS = [(i, j) for j in range(ITERS) for i in range(j + 1)] + [(ITERS - 1, ITERS)]
SLOT = {pair: at for at, pair in enumerate(PAIRS)}


def face(first, second):
    return 2.0 * first * second / (first + second)


def coefficients(gram):
    zero = jnp.zeros_like(gram(0, 0))
    one = zero + 1.0
    c_r, c_p = [one], [one]
    c_x = [zero] * ITERS
    r_dot = [gram(0, l) for l in range(ITERS)]
    rz = r_dot[0]
    for step in range(ITERS):
        c_q = [zero] * (step + 2)
        for i in range(step + 1):
            c_q[i] = c_q[i] + (1.0 - A[i]) * c_p[i]
            c_q[i + 1] = c_q[i + 1] - B[i + 1] * c_p[i]
            if i:
                c_q[i - 1] = c_q[i - 1] - B[i] * c_p[i]
        q_dot = {
            l: functools.reduce(lambda s, t: s + t, [c_q[i] * gram(i, l) for i in range(step + 2)])
            for l in range(step, ITERS)
        }
        alpha = rz / (c_r[step] * q_dot[step])
        c_x = [c_x[i] + alpha * c_p[i] if i <= step else c_x[i] for i in range(ITERS)]
        c_r = [(c_r[i] if i <= step else zero) - alpha * c_q[i] for i in range(step + 2)]
        if step + 1 < ITERS:
            r_dot = {l: r_dot[l] - alpha * q_dot[l] for l in range(step + 1, ITERS)}
            rz_new = c_r[step + 1] * r_dot[step + 1]
            beta = rz_new / rz
            rz = rz_new
            c_p = [c_r[i] + (beta * c_p[i] if i <= step else zero) for i in range(step + 2)]
    return c_x, c_r


def basis_kernel(
    dims,
    counts_hbm, sources_hbm, sigma_hbm, x_hbm, x_in, v, diag, table,
    counts, sources, sig, halo, sig_halo, weights, recip, rows_acc, last_acc, held_acc, parts,
    load_sem, sig_send, sig_recv, send_sem, recv_sem, part_send, part_recv, known_sem,
):
    slabs, ncol, depth, rows = dims
    cells = depth * rows
    plane = rows
    slab = lax.axis_index("slab")
    group = lax.axis_index("src")
    core = group % CORES
    twin = group - core + (CORES - 1 - core)
    left, right = (slab + slabs - 1) % slabs, (slab + 1) % slabs

    deep = slabs // RING
    here_z, here_x = slab // RING, slab % RING
    steps = [(dz, dx) for dz in range(deep) for dx in range(RING) if dz or dx]
    steps.sort(key=lambda step: -min(step[0], deep - step[0]) - min(step[1], RING - step[1]))
    others = [((here_z + dz) % deep) * RING + (here_x + dx) % RING for dz, dx in steps]
    body = pl.ds(PAD, cells)

    barrier = pltpu.get_barrier_semaphore()
    greeted = [(left, group), (right, group), (slab, twin)]
    for at in greeted:
        pl.semaphore_signal(barrier, inc=1, device_id=at, device_id_type=MESH)

    load_sig = pltpu.make_async_copy(sigma_hbm, sig.at[body], load_sem.at[0])
    load_sig.start()
    load_x = [pltpu.make_async_copy(x_hbm.at[c], x_in.at[c, body], load_sem.at[1 + c]) for c in range(ncol)]
    for copy in load_x:
        copy.start()
    load_ints = [
        pltpu.make_async_copy(counts_hbm, counts, load_sem.at[1 + ncol]),
        pltpu.make_async_copy(sources_hbm, sources, load_sem.at[2 + ncol]),
    ]
    for copy in load_ints:
        copy.start()

    pl.semaphore_wait(barrier, len(greeted))

    low_rows, high_rows = pl.ds(0, plane), pl.ds(cells - plane, plane)

    def remote(src, dst, send, recv, at, of=group):
        return pltpu.make_async_remote_copy(
            src_ref=src, dst_ref=dst, send_sem=send, recv_sem=recv, device_id=(at, of), device_id_type=MESH
        )

    edge = pl.ds(pl.multiple_of((1 - core) * (cells - plane), plane), plane)
    sig_out = remote(
        sigma_hbm.at[edge], sig_halo.at[core], sig_send.at[0], sig_recv.at[0],
        (slab + (1 - 2 * core) + slabs) % slabs,
    )
    sig_out.start()
    sig_share = remote(sig_halo.at[core], sig_halo.at[core], sig_send.at[1], sig_recv.at[1], slab, twin)

    def halo_copies(k, c):
        if k == 0:
            high, low = x_hbm.at[c, high_rows], x_hbm.at[c, low_rows]
        else:
            high = v.at[k - 1, c, pl.ds(PAD + cells - plane, plane)]
            low = v.at[k - 1, c, pl.ds(PAD, plane)]
        return (
            remote(high, halo.at[k, 0, c], send_sem.at[k, 0, c], recv_sem.at[k, 0, c], right),
            remote(low, halo.at[k, 1, c], send_sem.at[k, 1, c], recv_sem.at[k, 1, c], left),
        )

    for c in range(ncol):
        for copy in halo_copies(0, c):
            copy.start()

    blank = jnp.zeros((PAD, 128), jnp.float32)
    for c in range(ncol):
        x_in[c, pl.ds(0, PAD)] = blank
        x_in[c, pl.ds(PAD + cells, PAD)] = blank
        for k in range(STAGES):
            v[k, c, pl.ds(0, PAD)] = blank
            v[k, c, pl.ds(PAD + cells, PAD)] = blank
    sig[pl.ds(0, PAD)] = blank + 1.0
    sig[pl.ds(PAD + cells, PAD)] = blank + 1.0
    rows_acc[...] = jnp.zeros_like(rows_acc)
    last_acc[...] = jnp.zeros_like(last_acc)

    load_sig.wait()

    lane = lax.broadcasted_iota(jnp.int32, (CHUNK, 128), 1)
    sub = lax.broadcasted_iota(jnp.int32, (CHUNK, 128), 0)
    per_plane = plane // CHUNK

    def start_row(q):
        return pl.multiple_of(q * CHUNK, CHUNK)

    def set_weights(at, total, inner):
        inverse = 1.0 / total
        diag[at] = total
        recip[at] = inverse
        for i, w in enumerate(inner):
            weights[i, at] = w * inverse

    def weight_chunk(z, q):
        row = start_row(z * per_plane + q)
        at = pl.ds(row, CHUNK)
        own = sig[pl.ds(PAD + row, CHUNK)]
        x_at = sub + row % plane
        first_x, last_x = x_at == 0, x_at == plane - 1
        first_y, last_y = lane == 0, lane == 127
        others = [
            None if z == 0 else (sig[pl.ds(PAD + row - plane, CHUNK)], None),
            None if z == depth - 1 else (sig[pl.ds(PAD + row + plane, CHUNK)], None),
            (sig[pl.ds(PAD - 1 + row, CHUNK)], first_x),
            (sig[pl.ds(PAD + 1 + row, CHUNK)], last_x),
            (pltpu.roll(own, 1, 1), first_y),
            (pltpu.roll(own, 127, 1), last_y),
        ]
        total = None
        inner = {}
        for i, pair in enumerate(others):
            if pair is None:
                continue
            other, outside = pair
            w = face(own, other if outside is None else jnp.where(outside, own, other))
            total = w if total is None else total + w
            inner[i] = w if outside is None else jnp.where(outside, 0.0, w)
        if 0 < z < depth - 1:
            set_weights(at, total, [inner[i] for i in range(6)])
        else:
            diag[at] = total
            for i, w in inner.items():
                weights[i, at] = w

    def finish_chunk(z, q):
        side = 0 if z == 0 else 1
        row = start_row(z * per_plane + q)
        at = pl.ds(row, CHUNK)
        own = sig[pl.ds(PAD + row, CHUNK)]
        end = (slab == (0 if side == 0 else slabs - 1)).astype(jnp.int32)
        outside = (jnp.zeros((CHUNK, 128), jnp.int32) + end) > 0
        w = face(own, jnp.where(outside, own, sig_halo[side, pl.ds(start_row(q), CHUNK)]))
        inner = [weights[i, at] for i in range(6) if i != side]
        inner.insert(side, jnp.where(outside, 0.0, w))
        set_weights(at, diag[at] + w, inner)

    for z in [0, depth - 1, *range(1, depth - 1)]:
        lax.fori_loop(0, per_plane, lambda q, _, z=z: (weight_chunk(z, q), 0)[1], 0)
    sig_out.wait_recv()
    sig_share.start()
    sig_share.wait_recv()
    for z in (0, depth - 1):
        lax.fori_loop(0, per_plane, lambda q, _, z=z: (finish_chunk(z, q), 0)[1], 0)
    for copy in load_ints:
        copy.wait()

    def stage(k, c):
        def field(at):
            return x_in[c, at] if k == 0 else v[k - 1, c, at]

        firsts = range(k + 1)
        cell = sources[c, group] - slab * (cells * 128) if k == 0 else None

        def work(row, below, above):
            here = pl.ds(PAD + row, plane)
            at = pl.ds(row, plane)
            mid = field(here)
            image = (
                weights[0, at] * below
                + weights[1, at] * above
                + weights[2, at] * field(pl.ds(PAD - 1 + row, plane))
                + weights[3, at] * field(pl.ds(PAD + 1 + row, plane))
                + weights[4, at] * pltpu.roll(mid, 1, 1)
                + weights[5, at] * pltpu.roll(mid, 127, 1)
            )
            if k == 0:
                ids = (
                    lax.broadcasted_iota(jnp.int32, (plane, 128), 0) + row
                ) * 128 + lax.broadcasted_iota(jnp.int32, (plane, 128), 1)
                new = jnp.where(ids == cell, recip[at], 0.0) + (image - mid)
            else:
                j = k - 1
                new = (1.0 / B[k]) * image + (-A[j] / B[k]) * mid
                if j:
                    new = new + (-B[j] / B[k]) * v[k - 2, c, here]
            v[k, c, here] = new

        def dots(q, sums):
            row = start_row(q)
            here = pl.ds(PAD + row, CHUNK)
            scaled = diag[pl.ds(row, CHUNK)] * v[k, c, here]
            out = []
            for i, total in zip(firsts, sums):
                product = scaled * v[i, c, here]
                for part in range(CHUNK // 8):
                    total = total + product[part * 8:(part + 1) * 8]
                out.append(total)
            return tuple(out)

        def inside(z, _):
            row = pl.multiple_of(z * plane, plane)
            work(row, field(pl.ds(PAD + row - plane, plane)), field(pl.ds(PAD + row + plane, plane)))
            return 0

        lax.fori_loop(1, depth - 1, inside, 0)
        sums = tuple(jnp.zeros((8, 128), jnp.float32) for _ in firsts)
        sums = lax.fori_loop(per_plane, (depth - 1) * per_plane, dots, sums)

        from_left, from_right = halo_copies(k, c)
        to_right, to_left = halo_copies(k + 1, c)
        from_left.wait_recv()
        work(0, halo[k, 0, c], field(pl.ds(PAD + plane, plane)))
        if k == ITERS - 1:
            pl.when(c != ncol - 2)(lambda: to_left.start())

            @pl.when(c == ncol - 1)
            def _():
                halo_copies(k + 1, ncol - 2)[1].start()

        else:
            to_left.start()
        from_right.wait_recv()
        work(cells - plane, field(pl.ds(PAD + cells - 2 * plane, plane)), halo[k, 1, c])
        to_right.start()

        sums = lax.fori_loop(0, per_plane, dots, sums)
        sums = lax.fori_loop((depth - 1) * per_plane, depth * per_plane, dots, sums)
        for i, total in zip(firsts, sums):
            row = jnp.sum(total, axis=0, keepdims=True)
            rows_acc[pl.ds(SLOT[i, k] * ncol + c, 1), :] = row

    def fold(array):
        total = array[0:8]
        for part in range(8, plane, 8):
            total = total + array[part:part + 8]
        return total

    def last_plane(c, row, below, above):
        here, at = pl.ds(PAD + row, plane), pl.ds(row, plane)
        mid = v[ITERS - 1, c, here]
        image = (
            weights[2, at] * v[ITERS - 1, c, pl.ds(PAD - 1 + row, plane)]
            + weights[3, at] * v[ITERS - 1, c, pl.ds(PAD + 1 + row, plane)]
            + weights[4, at] * pltpu.roll(mid, 1, 1)
            + weights[5, at] * pltpu.roll(mid, 127, 1)
        )
        if below:
            image = image + weights[0, at] * v[ITERS - 1, c, pl.ds(PAD + row - plane, plane)]
        if above:
            image = image + weights[1, at] * v[ITERS - 1, c, pl.ds(PAD + row + plane, plane)]
        v[ITERS, c, here] = (
            (1.0 / B[ITERS]) * image
            + (-A[ITERS - 1] / B[ITERS]) * mid
            + (-B[ITERS - 1] / B[ITERS]) * v[ITERS - 2, c, here]
        )
        held_acc[c] = held_acc[c] + fold(diag[at] * mid * image)

    def last_inner(c, _):
        held_acc[c] = jnp.zeros((8, 128), jnp.float32)
        last_plane(c, 0, False, True)

        def inside(z, _):
            last_plane(c, pl.multiple_of(z * plane, plane), True, True)
            return 0

        lax.fori_loop(1, depth - 1, inside, 0)
        last_plane(c, cells - plane, True, False)
        return 0

    def last_edge(c, side, summed):
        halo_copies(ITERS, c)[side].wait_recv()
        row = 0 if side == 0 else cells - plane
        here, at = pl.ds(PAD + row, plane), pl.ds(row, plane)
        outer = weights[side, at] * halo[ITERS, side, c]
        v[ITERS, c, here] = v[ITERS, c, here] + (1.0 / B[ITERS]) * outer
        if summed:
            total = held_acc[c] + 2.0 * fold(diag[at] * v[ITERS - 1, c, here] * outer)
            last_acc[pl.ds(c, 1), :] = jnp.sum(total, axis=0, keepdims=True)

    reach = [4]
    while 2 * reach[-1] < slabs:
        reach.append(2 * reach[-1])
    rounds = reach[:-1]

    for k in range(STAGES):
        at_round = k - 4
        if 1 <= at_round <= len(rounds):
            for side in range(2):
                pl.semaphore_wait(known_sem.at[at_round - 1, side], 1)
        if 0 <= at_round < len(rounds):
            for side, far in enumerate((rounds[at_round], slabs - rounds[at_round])):
                pl.semaphore_signal(
                    known_sem.at[at_round, side], inc=1,
                    device_id=((slab + far) % slabs, group), device_id_type=MESH,
                )
        if k == ITERS:
            mine = jnp.sum(jnp.transpose(rows_acc[...]), axis=0, keepdims=True)
            lax.fori_loop(0, ncol, last_inner, 0)
            lax.fori_loop(0, ncol - 1, lambda c, _: (last_edge(c, 0, True), 0)[1], 0)
            last_edge(ncol - 1, 1, True)
            break

        def column(c, _, k=k):
            if k == 0:
                pltpu.make_async_copy(x_hbm.at[c], x_in.at[c, body], load_sem.at[1 + c]).wait()
            stage(k, c)
            return 0

        lax.fori_loop(0, ncol, column, 0)

    spot = SLOT[ITERS - 1, ITERS] * ncol + lax.broadcasted_iota(jnp.int32, (8, 128), 0)
    last = jnp.where(
        lax.broadcasted_iota(jnp.int32, (8, 128), 1) == spot, jnp.sum(last_acc[...], axis=1, keepdims=True), 0.0
    )
    parts[slab] = mine + jnp.sum(last, axis=0, keepdims=True)
    part_copies = [remote(parts.at[slab], parts.at[slab], part_send, part_recv, at) for at in others]
    for copy in part_copies:
        copy.start()
    last_edge(ncol - 1, 0, False)
    lax.fori_loop(0, ncol - 1, lambda c, _: (last_edge(c, 1, False), 0)[1], 0)
    sig_out.wait_send()
    sig_share.wait_send()
    for k in range(STAGES):
        def sent(c, _, k=k):
            for copy in halo_copies(k, c):
                copy.wait_send()
            return 0

        lax.fori_loop(0, ncol, sent, 0)
    every = parts.at[pl.ds(0, slabs - 1)]
    all_parts = remote(every, every, part_send, part_recv, right)
    all_parts.wait_recv()
    terms = [parts[i] for i in range(slabs)]
    while len(terms) > 1:
        terms = [sum(terms[i:i + 2][1:], terms[i]) for i in range(0, len(terms), 2)]
    total = terms[0]

    wide = jnp.broadcast_to(total, (8, 128))
    entries = {}
    for pair, at in SLOT.items():
        entries[pair] = wide if at == 0 else pltpu.roll(wide, 128 - at * ncol, 1)

    entries[(ITERS - 1, ITERS)] = (
        entries[(ITERS - 1, ITERS)]
        - A[ITERS - 1] * entries[(ITERS - 1, ITERS - 1)]
        - B[ITERS - 1] * entries[(ITERS - 2, ITERS - 1)]
    ) / B[ITERS]

    def gram(i, j):
        return entries[(i, j)] if i <= j and (i, j) in entries else entries[(j, i)]

    c_x, c_r = coefficients(gram)
    live = lax.broadcasted_iota(jnp.int32, (8, 128), 1) < counts[group]
    for j, value in enumerate(c_x + c_r):
        value = jnp.where(live, value, 0.0)
        for c in range(ncol):
            table[c, pl.ds(j, 1)] = jnp.broadcast_to(value[:1, c:c + 1], (1, 128))

    all_parts.wait_send()


def combine_kernel(dims, x_in, v, diag, table, pot_hbm, res_hbm, pot, res, out_sem):
    ncol, cells, plane = dims

    def out_copies(c, row):
        at = pl.ds(row, plane)
        return (
            pltpu.make_async_copy(pot.at[c, at], pot_hbm.at[c, at], out_sem.at[0, c, row // plane]),
            pltpu.make_async_copy(res.at[c, at], res_hbm.at[c, at], out_sem.at[1, c, row // plane]),
        )

    for c in range(ncol):
        def combine(z, _, c=c):
            row = pl.multiple_of(z * plane, plane)
            here, at = pl.ds(PAD + row, plane), pl.ds(row, plane)
            new_x, new_r = x_in[c, here], None
            for j in range(STAGES):
                vec = v[j, c, here]
                if j < ITERS:
                    new_x = new_x + table[c, pl.ds(j, 1)] * vec
                term = table[c, pl.ds(ITERS + j, 1)] * vec
                new_r = term if new_r is None else new_r + term
            pot[c, at] = new_x
            res[c, at] = diag[at] * new_r
            for copy in out_copies(c, row):
                copy.start()
            return 0

        lax.fori_loop(0, cells // plane, combine, 0)
    for c in range(ncol):
        for row in range(0, cells, plane):
            for copy in out_copies(c, row):
                copy.wait()


def solution(mesh):
    slabs = mesh.shape["slab"]

    def shards(sigma, iterate, counts, sources):
        depth, rows, lanes = sigma.shape
        ncol = iterate.shape[0]
        cells = depth * rows
        f32 = jnp.float32
        vmem = pltpu.VMEM
        dma = pltpu.SemaphoreType.DMA
        anywhere = pl.BlockSpec(memory_space=pl.ANY)
        on_chip = pl.BlockSpec(memory_space=pltpu.VMEM)

        def in_hbm(array):
            return pltpu.with_memory_space_constraint(array, pltpu.HBM)

        sources = sources.T
        held = pl.pallas_call(
            functools.partial(basis_kernel, (slabs, ncol, depth, rows)),
            out_shape=(
                vmem((ncol, cells + 2 * PAD, lanes), f32),
                vmem((STAGES, ncol, cells + 2 * PAD, lanes), f32),
                vmem((cells, lanes), f32),
                vmem((ncol, 16, lanes), f32),
            ),
            in_specs=[anywhere] * 4,
            out_specs=(on_chip,) * 4,
            scratch_shapes=[
                pltpu.SMEM(counts.shape, jnp.int32),
                pltpu.SMEM(sources.shape, jnp.int32),
                vmem((cells + 2 * PAD, lanes), f32),
                vmem((STAGES, 2, ncol, rows, lanes), f32),
                vmem((2, rows, lanes), f32),
                vmem((6, cells, lanes), f32),
                vmem((cells, lanes), f32),
                vmem((128, 128), f32),
                vmem((8, 128), f32),
                vmem((ncol, 8, 128), f32),
                vmem((slabs, 1, 128), f32),
                dma((3 + ncol,)),
                dma((2,)),
                dma((2,)),
                dma((STAGES, 2, ncol)),
                dma((STAGES, 2, ncol)),
                dma,
                dma,
                pltpu.SemaphoreType.REGULAR((2, 2)),
            ],
            compiler_params=pltpu.CompilerParams(
                collective_id=0, has_side_effects=True, vmem_limit_bytes=24 * 1024 * 1024
            ),
        )(
            in_hbm(counts),
            in_hbm(sources),
            in_hbm(sigma.reshape(cells, lanes)),
            in_hbm(iterate.reshape(ncol, cells, lanes)),
        )
        flat = pltpu.HBM((ncol, cells, lanes), f32)
        potential, residual = pl.pallas_call(
            functools.partial(combine_kernel, (ncol, cells, rows)),
            out_shape=(flat, flat),
            in_specs=[on_chip] * 4,
            out_specs=(anywhere, anywhere),
            scratch_shapes=[vmem((ncol, cells, lanes), f32), vmem((ncol, cells, lanes), f32), dma((2, ncol, depth))],
            compiler_params=pltpu.CompilerParams(vmem_limit_bytes=24 * 1024 * 1024),
        )(*held)
        return potential.reshape(iterate.shape), residual.reshape(iterate.shape)

    return jax.shard_map(
        shards,
        mesh=mesh,
        in_specs=(P("slab", None, None), P("src", "slab", None, None), P(), P()),
        out_specs=(P("src", "slab", None, None), P("src", "slab", None, None)),
        check_vma=False,
    )
```

```python
import functools

import jax
import jax.numpy as jnp
from jax import lax
from jax.experimental import pallas as pl
from jax.experimental.pallas import tpu as pltpu
from jax.sharding import PartitionSpec as P

MESH = pl.DeviceIdType.MESH
ITERS = 6
STAGES = ITERS + 1
RING = 4
CORES = 2
PAD = 8
CHUNK = 64

A = (-0.1666, -0.13, -0.07, -0.02, -0.02, -0.01)
B = (0.0, 0.373, 0.458, 0.484, 0.487, 0.493, 0.495)

PAIRS = [(i, j) for j in range(ITERS) for i in range(j + 1)] + [(ITERS - 1, ITERS)]
SLOT = {pair: at for at, pair in enumerate(PAIRS)}


def face(first, second):
    return 2.0 * first * second / (first + second)


def coefficients(gram):
    zero = jnp.zeros_like(gram(0, 0))
    one = zero + 1.0
    c_r, c_p = [one], [one]
    c_x = [zero] * ITERS
    r_dot = [gram(0, l) for l in range(ITERS)]
    rz = r_dot[0]
    for step in range(ITERS):
        c_q = [zero] * (step + 2)
        for i in range(step + 1):
            c_q[i] = c_q[i] + (1.0 - A[i]) * c_p[i]
            c_q[i + 1] = c_q[i + 1] - B[i + 1] * c_p[i]
            if i:
                c_q[i - 1] = c_q[i - 1] - B[i] * c_p[i]
        q_dot = {
            l: functools.reduce(lambda s, t: s + t, [c_q[i] * gram(i, l) for i in range(step + 2)])
            for l in range(step, ITERS)
        }
        alpha = rz / (c_r[step] * q_dot[step])
        c_x = [c_x[i] + alpha * c_p[i] if i <= step else c_x[i] for i in range(ITERS)]
        c_r = [(c_r[i] if i <= step else zero) - alpha * c_q[i] for i in range(step + 2)]
        if step + 1 < ITERS:
            r_dot = {l: r_dot[l] - alpha * q_dot[l] for l in range(step + 1, ITERS)}
            rz_new = c_r[step + 1] * r_dot[step + 1]
            beta = rz_new / rz
            rz = rz_new
            c_p = [c_r[i] + (beta * c_p[i] if i <= step else zero) for i in range(step + 2)]
    return c_x, c_r


def basis_kernel(
    dims,
    counts_hbm, sources_hbm, sigma_hbm, x_hbm, x_in, v, diag, table,
    counts, sources, sig, halo, sig_halo, weights, recip, rows_acc, last_acc, held_acc, parts,
    load_sem, sig_send, sig_recv, send_sem, recv_sem, part_send, part_recv, known_sem,
):
    slabs, ncol, depth, rows = dims
    cells = depth * rows
    plane = rows
    slab = lax.axis_index("slab")
    group = lax.axis_index("src")
    core = group % CORES
    twin = group - core + (CORES - 1 - core)
    left, right = (slab + slabs - 1) % slabs, (slab + 1) % slabs

    deep = slabs // RING
    here_z, here_x = slab // RING, slab % RING
    steps = [(dz, dx) for dz in range(deep) for dx in range(RING) if dz or dx]
    steps.sort(key=lambda step: -min(step[0], deep - step[0]) - min(step[1], RING - step[1]))
    others = [((here_z + dz) % deep) * RING + (here_x + dx) % RING for dz, dx in steps]
    body = pl.ds(PAD, cells)

    barrier = pltpu.get_barrier_semaphore()
    greeted = [(left, group), (right, group), (slab, twin)]
    for at in greeted:
        pl.semaphore_signal(barrier, inc=1, device_id=at, device_id_type=MESH)

    load_sig = pltpu.make_async_copy(sigma_hbm, sig.at[body], load_sem.at[0])
    load_sig.start()
    load_x = [pltpu.make_async_copy(x_hbm.at[c], x_in.at[c, body], load_sem.at[1 + c]) for c in range(ncol)]
    for copy in load_x:
        copy.start()
    load_ints = [
        pltpu.make_async_copy(counts_hbm, counts, load_sem.at[1 + ncol]),
        pltpu.make_async_copy(sources_hbm, sources, load_sem.at[2 + ncol]),
    ]
    for copy in load_ints:
        copy.start()

    pl.semaphore_wait(barrier, len(greeted))

    low_rows, high_rows = pl.ds(0, plane), pl.ds(cells - plane, plane)

    def remote(src, dst, send, recv, at, of=group):
        return pltpu.make_async_remote_copy(
            src_ref=src, dst_ref=dst, send_sem=send, recv_sem=recv, device_id=(at, of), device_id_type=MESH
        )

    edge = pl.ds(pl.multiple_of((1 - core) * (cells - plane), plane), plane)
    sig_out = remote(
        sigma_hbm.at[edge], sig_halo.at[core], sig_send.at[0], sig_recv.at[0],
        (slab + (1 - 2 * core) + slabs) % slabs,
    )
    sig_out.start()
    sig_share = remote(sig_halo.at[core], sig_halo.at[core], sig_send.at[1], sig_recv.at[1], slab, twin)

    def halo_copies(k, c):
        if k == 0:
            high, low = x_hbm.at[c, high_rows], x_hbm.at[c, low_rows]
        else:
            high = v.at[k - 1, c, pl.ds(PAD + cells - plane, plane)]
            low = v.at[k - 1, c, pl.ds(PAD, plane)]
        return (
            remote(high, halo.at[k, 0, c], send_sem.at[k, 0, c], recv_sem.at[k, 0, c], right),
            remote(low, halo.at[k, 1, c], send_sem.at[k, 1, c], recv_sem.at[k, 1, c], left),
        )

    for c in range(ncol):
        for copy in halo_copies(0, c):
            copy.start()

    blank = jnp.zeros((PAD, 128), jnp.float32)
    for c in range(ncol):
        x_in[c, pl.ds(0, PAD)] = blank
        x_in[c, pl.ds(PAD + cells, PAD)] = blank
        for k in range(STAGES):
            v[k, c, pl.ds(0, PAD)] = blank
            v[k, c, pl.ds(PAD + cells, PAD)] = blank
    sig[pl.ds(0, PAD)] = blank + 1.0
    sig[pl.ds(PAD + cells, PAD)] = blank + 1.0
    rows_acc[...] = jnp.zeros_like(rows_acc)
    last_acc[...] = jnp.zeros_like(last_acc)

    load_sig.wait()

    lane = lax.broadcasted_iota(jnp.int32, (CHUNK, 128), 1)
    sub = lax.broadcasted_iota(jnp.int32, (CHUNK, 128), 0)
    per_plane = plane // CHUNK

    def start_row(q):
        return pl.multiple_of(q * CHUNK, CHUNK)

    def set_weights(at, total, inner):
        inverse = 1.0 / total
        diag[at] = total
        recip[at] = inverse
        for i, w in enumerate(inner):
            weights[i, at] = w * inverse

    def weight_chunk(z, q):
        row = start_row(z * per_plane + q)
        at = pl.ds(row, CHUNK)
        own = sig[pl.ds(PAD + row, CHUNK)]
        x_at = sub + row % plane
        first_x, last_x = x_at == 0, x_at == plane - 1
        first_y, last_y = lane == 0, lane == 127
        others = [
            None if z == 0 else (sig[pl.ds(PAD + row - plane, CHUNK)], None),
            None if z == depth - 1 else (sig[pl.ds(PAD + row + plane, CHUNK)], None),
            (sig[pl.ds(PAD - 1 + row, CHUNK)], first_x),
            (sig[pl.ds(PAD + 1 + row, CHUNK)], last_x),
            (pltpu.roll(own, 1, 1), first_y),
            (pltpu.roll(own, 127, 1), last_y),
        ]
        total = None
        inner = {}
        for i, pair in enumerate(others):
            if pair is None:
                continue
            other, outside = pair
            w = face(own, other if outside is None else jnp.where(outside, own, other))
            total = w if total is None else total + w
            inner[i] = w if outside is None else jnp.where(outside, 0.0, w)
        if 0 < z < depth - 1:
            set_weights(at, total, [inner[i] for i in range(6)])
        else:
            diag[at] = total
            for i, w in inner.items():
                weights[i, at] = w

    def finish_chunk(z, q):
        side = 0 if z == 0 else 1
        row = start_row(z * per_plane + q)
        at = pl.ds(row, CHUNK)
        own = sig[pl.ds(PAD + row, CHUNK)]
        end = (slab == (0 if side == 0 else slabs - 1)).astype(jnp.int32)
        outside = (jnp.zeros((CHUNK, 128), jnp.int32) + end) > 0
        w = face(own, jnp.where(outside, own, sig_halo[side, pl.ds(start_row(q), CHUNK)]))
        inner = [weights[i, at] for i in range(6) if i != side]
        inner.insert(side, jnp.where(outside, 0.0, w))
        set_weights(at, diag[at] + w, inner)

    for z in [0, depth - 1, *range(1, depth - 1)]:
        lax.fori_loop(0, per_plane, lambda q, _, z=z: (weight_chunk(z, q), 0)[1], 0)
    sig_out.wait_recv()
    sig_share.start()
    sig_share.wait_recv()
    for z in (0, depth - 1):
        lax.fori_loop(0, per_plane, lambda q, _, z=z: (finish_chunk(z, q), 0)[1], 0)
    for copy in load_ints:
        copy.wait()

    def stage(k, c):
        def field(at):
            return x_in[c, at] if k == 0 else v[k - 1, c, at]

        firsts = range(k + 1)
        cell = sources[c, group] - slab * (cells * 128) if k == 0 else None

        def work(row, below, above):
            here = pl.ds(PAD + row, plane)
            at = pl.ds(row, plane)
            mid = field(here)
            image = (
                weights[0, at] * below
                + weights[1, at] * above
                + weights[2, at] * field(pl.ds(PAD - 1 + row, plane))
                + weights[3, at] * field(pl.ds(PAD + 1 + row, plane))
                + weights[4, at] * pltpu.roll(mid, 1, 1)
                + weights[5, at] * pltpu.roll(mid, 127, 1)
            )
            if k == 0:
                ids = (
                    lax.broadcasted_iota(jnp.int32, (plane, 128), 0) + row
                ) * 128 + lax.broadcasted_iota(jnp.int32, (plane, 128), 1)
                new = jnp.where(ids == cell, recip[at], 0.0) + (image - mid)
            else:
                j = k - 1
                new = (1.0 / B[k]) * image + (-A[j] / B[k]) * mid
                if j:
                    new = new + (-B[j] / B[k]) * v[k - 2, c, here]
            v[k, c, here] = new

        def dots(q, sums):
            row = start_row(q)
            here = pl.ds(PAD + row, CHUNK)
            scaled = diag[pl.ds(row, CHUNK)] * v[k, c, here]
            out = []
            for i, total in zip(firsts, sums):
                product = scaled * v[i, c, here]
                for part in range(CHUNK // 8):
                    total = total + product[part * 8:(part + 1) * 8]
                out.append(total)
            return tuple(out)

        def inside(z, _):
            row = pl.multiple_of(z * plane, plane)
            work(row, field(pl.ds(PAD + row - plane, plane)), field(pl.ds(PAD + row + plane, plane)))
            return 0

        lax.fori_loop(1, depth - 1, inside, 0)
        sums = tuple(jnp.zeros((8, 128), jnp.float32) for _ in firsts)
        sums = lax.fori_loop(per_plane, (depth - 1) * per_plane, dots, sums)

        from_left, from_right = halo_copies(k, c)
        to_right, to_left = halo_copies(k + 1, c)
        from_left.wait_recv()
        work(0, halo[k, 0, c], field(pl.ds(PAD + plane, plane)))
        if k == ITERS - 1:
            pl.when(c != ncol - 2)(lambda: to_left.start())

            @pl.when(c == ncol - 1)
            def _():
                halo_copies(k + 1, ncol - 2)[1].start()

        else:
            to_left.start()
        from_right.wait_recv()
        work(cells - plane, field(pl.ds(PAD + cells - 2 * plane, plane)), halo[k, 1, c])
        to_right.start()

        sums = lax.fori_loop(0, per_plane, dots, sums)
        sums = lax.fori_loop((depth - 1) * per_plane, depth * per_plane, dots, sums)
        for i, total in zip(firsts, sums):
            row = jnp.sum(total, axis=0, keepdims=True)
            rows_acc[pl.ds(SLOT[i, k] * ncol + c, 1), :] = row

    def fold(array):
        total = array[0:8]
        for part in range(8, plane, 8):
            total = total + array[part:part + 8]
        return total

    def last_plane(c, row, below, above):
        here, at = pl.ds(PAD + row, plane), pl.ds(row, plane)
        mid = v[ITERS - 1, c, here]
        image = (
            weights[2, at] * v[ITERS - 1, c, pl.ds(PAD - 1 + row, plane)]
            + weights[3, at] * v[ITERS - 1, c, pl.ds(PAD + 1 + row, plane)]
            + weights[4, at] * pltpu.roll(mid, 1, 1)
            + weights[5, at] * pltpu.roll(mid, 127, 1)
        )
        if below:
            image = image + weights[0, at] * v[ITERS - 1, c, pl.ds(PAD + row - plane, plane)]
        if above:
            image = image + weights[1, at] * v[ITERS - 1, c, pl.ds(PAD + row + plane, plane)]
        v[ITERS, c, here] = (
            (1.0 / B[ITERS]) * image
            + (-A[ITERS - 1] / B[ITERS]) * mid
            + (-B[ITERS - 1] / B[ITERS]) * v[ITERS - 2, c, here]
        )
        held_acc[c] = held_acc[c] + fold(diag[at] * mid * image)

    def sent(k, c):
        for copy in halo_copies(k, c):
            copy.wait_send()

    def last_inner(c, _):
        held_acc[c] = jnp.zeros((8, 128), jnp.float32)
        last_plane(c, 0, False, True)

        def inside(z, _):
            last_plane(c, pl.multiple_of(z * plane, plane), True, True)
            return 0

        lax.fori_loop(1, depth - 1, inside, 0)
        last_plane(c, cells - plane, True, False)
        return 0

    def last_edge(c, side, summed):
        halo_copies(ITERS, c)[side].wait_recv()
        row = 0 if side == 0 else cells - plane
        here, at = pl.ds(PAD + row, plane), pl.ds(row, plane)
        outer = weights[side, at] * halo[ITERS, side, c]
        v[ITERS, c, here] = v[ITERS, c, here] + (1.0 / B[ITERS]) * outer
        if summed:
            total = held_acc[c] + 2.0 * fold(diag[at] * v[ITERS - 1, c, here] * outer)
            last_acc[pl.ds(c, 1), :] = jnp.sum(total, axis=0, keepdims=True)

    reach = [4]
    while 2 * reach[-1] < slabs:
        reach.append(2 * reach[-1])
    rounds = reach[:-1]

    for k in range(STAGES):
        at_round = k - 4
        if 1 <= at_round <= len(rounds):
            for side in range(2):
                pl.semaphore_wait(known_sem.at[at_round - 1, side], 1)
        if 0 <= at_round < len(rounds):
            for side, far in enumerate((rounds[at_round], slabs - rounds[at_round])):
                pl.semaphore_signal(
                    known_sem.at[at_round, side], inc=1,
                    device_id=((slab + far) % slabs, group), device_id_type=MESH,
                )
        if k == ITERS:
            mine = jnp.sum(jnp.transpose(rows_acc[...]), axis=0, keepdims=True)
            lax.fori_loop(0, ncol, last_inner, 0)
            for done in range(ITERS):
                lax.fori_loop(0, ncol, lambda c, _, done=done: (sent(done, c), 0)[1], 0)
            lax.fori_loop(0, ncol - 1, lambda c, _: (last_edge(c, 0, True), 0)[1], 0)
            last_edge(ncol - 1, 1, True)
            break

        def column(c, _, k=k):
            if k == 0:
                pltpu.make_async_copy(x_hbm.at[c], x_in.at[c, body], load_sem.at[1 + c]).wait()
            stage(k, c)
            return 0

        lax.fori_loop(0, ncol, column, 0)

    spot = SLOT[ITERS - 1, ITERS] * ncol + lax.broadcasted_iota(jnp.int32, (8, 128), 0)
    last = jnp.where(
        lax.broadcasted_iota(jnp.int32, (8, 128), 1) == spot, jnp.sum(last_acc[...], axis=1, keepdims=True), 0.0
    )
    parts[slab] = mine + jnp.sum(last, axis=0, keepdims=True)
    part_copies = [remote(parts.at[slab], parts.at[slab], part_send, part_recv, at) for at in others]
    for copy in part_copies:
        copy.start()
    last_edge(ncol - 1, 0, False)
    lax.fori_loop(0, ncol - 1, lambda c, _: (last_edge(c, 1, False), 0)[1], 0)
    sig_out.wait_send()
    sig_share.wait_send()
    lax.fori_loop(0, ncol, lambda c, _: (sent(ITERS, c), 0)[1], 0)
    every = parts.at[pl.ds(0, slabs - 1)]
    all_parts = remote(every, every, part_send, part_recv, right)
    all_parts.wait_recv()
    terms = [parts[i] for i in range(slabs)]
    while len(terms) > 1:
        terms = [sum(terms[i:i + 2][1:], terms[i]) for i in range(0, len(terms), 2)]
    total = terms[0]

    wide = jnp.broadcast_to(total, (8, 128))
    entries = {}
    for pair, at in SLOT.items():
        entries[pair] = wide if at == 0 else pltpu.roll(wide, 128 - at * ncol, 1)

    entries[(ITERS - 1, ITERS)] = (
        entries[(ITERS - 1, ITERS)]
        - A[ITERS - 1] * entries[(ITERS - 1, ITERS - 1)]
        - B[ITERS - 1] * entries[(ITERS - 2, ITERS - 1)]
    ) / B[ITERS]

    def gram(i, j):
        return entries[(i, j)] if i <= j and (i, j) in entries else entries[(j, i)]

    c_x, c_r = coefficients(gram)
    live = lax.broadcasted_iota(jnp.int32, (8, 128), 1) < counts[group]
    for j, value in enumerate(c_x + c_r):
        value = jnp.where(live, value, 0.0)
        for c in range(ncol):
            table[c, pl.ds(j, 1)] = jnp.broadcast_to(value[:1, c:c + 1], (1, 128))

    all_parts.wait_send()


def combine_kernel(dims, x_in, v, diag, table, pot_hbm, res_hbm, pot, res, out_sem):
    ncol, cells, plane = dims

    def out_copies(c, row):
        at = pl.ds(row, plane)
        return (
            pltpu.make_async_copy(pot.at[c, at], pot_hbm.at[c, at], out_sem.at[0, c, row // plane]),
            pltpu.make_async_copy(res.at[c, at], res_hbm.at[c, at], out_sem.at[1, c, row // plane]),
        )

    for c in range(ncol):
        def combine(z, _, c=c):
            row = pl.multiple_of(z * plane, plane)
            here, at = pl.ds(PAD + row, plane), pl.ds(row, plane)
            new_x, new_r = x_in[c, here], None
            for j in range(STAGES):
                vec = v[j, c, here]
                if j < ITERS:
                    new_x = new_x + table[c, pl.ds(j, 1)] * vec
                term = table[c, pl.ds(ITERS + j, 1)] * vec
                new_r = term if new_r is None else new_r + term
            pot[c, at] = new_x
            res[c, at] = diag[at] * new_r
            for copy in out_copies(c, row):
                copy.start()
            return 0

        lax.fori_loop(0, cells // plane, combine, 0)
    for c in range(ncol):
        for row in range(0, cells, plane):
            for copy in out_copies(c, row):
                copy.wait()


def solution(mesh):
    slabs = mesh.shape["slab"]

    def shards(sigma, iterate, counts, sources):
        depth, rows, lanes = sigma.shape
        ncol = iterate.shape[0]
        cells = depth * rows
        f32 = jnp.float32
        vmem = pltpu.VMEM
        dma = pltpu.SemaphoreType.DMA
        anywhere = pl.BlockSpec(memory_space=pl.ANY)
        on_chip = pl.BlockSpec(memory_space=pltpu.VMEM)

        def in_hbm(array):
            return pltpu.with_memory_space_constraint(array, pltpu.HBM)

        sources = sources.T
        held = pl.pallas_call(
            functools.partial(basis_kernel, (slabs, ncol, depth, rows)),
            out_shape=(
                vmem((ncol, cells + 2 * PAD, lanes), f32),
                vmem((STAGES, ncol, cells + 2 * PAD, lanes), f32),
                vmem((cells, lanes), f32),
                vmem((ncol, 16, lanes), f32),
            ),
            in_specs=[anywhere] * 4,
            out_specs=(on_chip,) * 4,
            scratch_shapes=[
                pltpu.SMEM(counts.shape, jnp.int32),
                pltpu.SMEM(sources.shape, jnp.int32),
                vmem((cells + 2 * PAD, lanes), f32),
                vmem((STAGES, 2, ncol, rows, lanes), f32),
                vmem((2, rows, lanes), f32),
                vmem((6, cells, lanes), f32),
                vmem((cells, lanes), f32),
                vmem((128, 128), f32),
                vmem((8, 128), f32),
                vmem((ncol, 8, 128), f32),
                vmem((slabs, 1, 128), f32),
                dma((3 + ncol,)),
                dma((2,)),
                dma((2,)),
                dma((STAGES, 2, ncol)),
                dma((STAGES, 2, ncol)),
                dma,
                dma,
                pltpu.SemaphoreType.REGULAR((2, 2)),
            ],
            compiler_params=pltpu.CompilerParams(
                collective_id=0, has_side_effects=True, vmem_limit_bytes=24 * 1024 * 1024
            ),
        )(
            in_hbm(counts),
            in_hbm(sources),
            in_hbm(sigma.reshape(cells, lanes)),
            in_hbm(iterate.reshape(ncol, cells, lanes)),
        )
        flat = pltpu.HBM((ncol, cells, lanes), f32)
        potential, residual = pl.pallas_call(
            functools.partial(combine_kernel, (ncol, cells, rows)),
            out_shape=(flat, flat),
            in_specs=[on_chip] * 4,
            out_specs=(anywhere, anywhere),
            scratch_shapes=[vmem((ncol, cells, lanes), f32), vmem((ncol, cells, lanes), f32), dma((2, ncol, depth))],
            compiler_params=pltpu.CompilerParams(vmem_limit_bytes=24 * 1024 * 1024),
        )(*held)
        return potential.reshape(iterate.shape), residual.reshape(iterate.shape)

    return jax.shard_map(
        shards,
        mesh=mesh,
        in_specs=(P("slab", None, None), P("src", "slab", None, None), P(), P()),
        out_specs=(P("src", "slab", None, None), P("src", "slab", None, None)),
        check_vma=False,
    )
```

```python
import functools

import jax
import jax.numpy as jnp
from jax import lax
from jax.experimental import pallas as pl
from jax.experimental.pallas import tpu as pltpu
from jax.sharding import PartitionSpec as P

MESH = pl.DeviceIdType.MESH
ITERS = 6
STAGES = ITERS + 1
RING = 4
CORES = 2
PAD = 8
CHUNK = 64

A = (-0.1666, -0.13, -0.07, -0.02, -0.02, -0.01)
B = (0.0, 0.373, 0.458, 0.484, 0.487, 0.493, 0.495)

PAIRS = [(i, j) for j in range(ITERS) for i in range(j + 1)] + [(ITERS - 1, ITERS)]
SLOT = {pair: at for at, pair in enumerate(PAIRS)}


def face(first, second):
    return 2.0 * first * second / (first + second)


def coefficients(gram):
    zero = jnp.zeros_like(gram(0, 0))
    one = zero + 1.0
    c_r, c_p = [one], [one]
    c_x = [zero] * ITERS
    r_dot = [gram(0, l) for l in range(ITERS)]
    rz = r_dot[0]
    for step in range(ITERS):
        c_q = [zero] * (step + 2)
        for i in range(step + 1):
            c_q[i] = c_q[i] + (1.0 - A[i]) * c_p[i]
            c_q[i + 1] = c_q[i + 1] - B[i + 1] * c_p[i]
            if i:
                c_q[i - 1] = c_q[i - 1] - B[i] * c_p[i]
        q_dot = {
            l: functools.reduce(lambda s, t: s + t, [c_q[i] * gram(i, l) for i in range(step + 2)])
            for l in range(step, ITERS)
        }
        alpha = rz / (c_r[step] * q_dot[step])
        c_x = [c_x[i] + alpha * c_p[i] if i <= step else c_x[i] for i in range(ITERS)]
        c_r = [(c_r[i] if i <= step else zero) - alpha * c_q[i] for i in range(step + 2)]
        if step + 1 < ITERS:
            r_dot = {l: r_dot[l] - alpha * q_dot[l] for l in range(step + 1, ITERS)}
            rz_new = c_r[step + 1] * r_dot[step + 1]
            beta = rz_new / rz
            rz = rz_new
            c_p = [c_r[i] + (beta * c_p[i] if i <= step else zero) for i in range(step + 2)]
    return c_x, c_r


def basis_kernel(
    dims,
    counts_hbm, sources_hbm, sigma_hbm, x_hbm, x_in, v, diag, table,
    counts, sources, sig, halo, sig_halo, weights, recip, rows_acc, last_acc, held_acc, parts,
    load_sem, sig_send, sig_recv, send_sem, recv_sem, part_send, part_recv, known_sem,
):
    slabs, ncol, depth, rows = dims
    cells = depth * rows
    plane = rows
    slab = lax.axis_index("slab")
    group = lax.axis_index("src")
    core = group % CORES
    twin = group - core + (CORES - 1 - core)
    left, right = (slab + slabs - 1) % slabs, (slab + 1) % slabs

    deep = slabs // RING
    here_z, here_x = slab // RING, slab % RING
    steps = [(dz, dx) for dz in range(deep) for dx in range(RING) if dz or dx]
    steps.sort(key=lambda step: -min(step[0], deep - step[0]) - min(step[1], RING - step[1]))
    others = [((here_z + dz) % deep) * RING + (here_x + dx) % RING for dz, dx in steps]
    body = pl.ds(PAD, cells)

    barrier = pltpu.get_barrier_semaphore()
    greeted = [(left, group), (right, group), (slab, twin)]
    for at in greeted:
        pl.semaphore_signal(barrier, inc=1, device_id=at, device_id_type=MESH)

    load_sig = pltpu.make_async_copy(sigma_hbm, sig.at[body], load_sem.at[0])
    load_sig.start()
    load_x = [pltpu.make_async_copy(x_hbm.at[c], x_in.at[c, body], load_sem.at[1 + c]) for c in range(ncol)]
    for copy in load_x:
        copy.start()
    load_ints = [
        pltpu.make_async_copy(counts_hbm, counts, load_sem.at[1 + ncol]),
        pltpu.make_async_copy(sources_hbm, sources, load_sem.at[2 + ncol]),
    ]
    for copy in load_ints:
        copy.start()

    pl.semaphore_wait(barrier, len(greeted))

    low_rows, high_rows = pl.ds(0, plane), pl.ds(cells - plane, plane)

    def remote(src, dst, send, recv, at, of=group):
        return pltpu.make_async_remote_copy(
            src_ref=src, dst_ref=dst, send_sem=send, recv_sem=recv, device_id=(at, of), device_id_type=MESH
        )

    edge = pl.ds(pl.multiple_of((1 - core) * (cells - plane), plane), plane)
    sig_out = remote(
        sigma_hbm.at[edge], sig_halo.at[core], sig_send.at[0], sig_recv.at[0],
        (slab + (1 - 2 * core) + slabs) % slabs,
    )
    sig_out.start()
    sig_share = remote(sig_halo.at[core], sig_halo.at[core], sig_send.at[1], sig_recv.at[1], slab, twin)

    def halo_copies(k, c):
        if k == 0:
            high, low = x_hbm.at[c, high_rows], x_hbm.at[c, low_rows]
        else:
            high = v.at[k - 1, c, pl.ds(PAD + cells - plane, plane)]
            low = v.at[k - 1, c, pl.ds(PAD, plane)]
        return (
            remote(high, halo.at[k, 0, c], send_sem.at[k, 0, c], recv_sem.at[k, 0, c], right),
            remote(low, halo.at[k, 1, c], send_sem.at[k, 1, c], recv_sem.at[k, 1, c], left),
        )

    for c in range(ncol):
        for copy in halo_copies(0, c):
            copy.start()

    blank = jnp.zeros((PAD, 128), jnp.float32)
    for c in range(ncol):
        x_in[c, pl.ds(0, PAD)] = blank
        x_in[c, pl.ds(PAD + cells, PAD)] = blank
        for k in range(STAGES):
            v[k, c, pl.ds(0, PAD)] = blank
            v[k, c, pl.ds(PAD + cells, PAD)] = blank
    sig[pl.ds(0, PAD)] = blank + 1.0
    sig[pl.ds(PAD + cells, PAD)] = blank + 1.0
    rows_acc[...] = jnp.zeros_like(rows_acc)
    last_acc[...] = jnp.zeros_like(last_acc)

    load_sig.wait()

    lane = lax.broadcasted_iota(jnp.int32, (CHUNK, 128), 1)
    sub = lax.broadcasted_iota(jnp.int32, (CHUNK, 128), 0)
    per_plane = plane // CHUNK

    def start_row(q):
        return pl.multiple_of(q * CHUNK, CHUNK)

    def set_weights(at, total, inner):
        inverse = 1.0 / total
        diag[at] = total
        recip[at] = inverse
        for i, w in enumerate(inner):
            weights[i, at] = w * inverse

    def weight_chunk(z, q):
        row = start_row(z * per_plane + q)
        at = pl.ds(row, CHUNK)
        own = sig[pl.ds(PAD + row, CHUNK)]
        x_at = sub + row % plane
        first_x, last_x = x_at == 0, x_at == plane - 1
        first_y, last_y = lane == 0, lane == 127
        others = [
            None if z == 0 else (sig[pl.ds(PAD + row - plane, CHUNK)], None),
            None if z == depth - 1 else (sig[pl.ds(PAD + row + plane, CHUNK)], None),
            (sig[pl.ds(PAD - 1 + row, CHUNK)], first_x),
            (sig[pl.ds(PAD + 1 + row, CHUNK)], last_x),
            (pltpu.roll(own, 1, 1), first_y),
            (pltpu.roll(own, 127, 1), last_y),
        ]
        total = None
        inner = {}
        for i, pair in enumerate(others):
            if pair is None:
                continue
            other, outside = pair
            w = face(own, other if outside is None else jnp.where(outside, own, other))
            total = w if total is None else total + w
            inner[i] = w if outside is None else jnp.where(outside, 0.0, w)
        if 0 < z < depth - 1:
            set_weights(at, total, [inner[i] for i in range(6)])
        else:
            diag[at] = total
            for i, w in inner.items():
                weights[i, at] = w

    def finish_chunk(z, q):
        side = 0 if z == 0 else 1
        row = start_row(z * per_plane + q)
        at = pl.ds(row, CHUNK)
        own = sig[pl.ds(PAD + row, CHUNK)]
        end = (slab == (0 if side == 0 else slabs - 1)).astype(jnp.int32)
        outside = (jnp.zeros((CHUNK, 128), jnp.int32) + end) > 0
        w = face(own, jnp.where(outside, own, sig_halo[side, pl.ds(start_row(q), CHUNK)]))
        inner = [weights[i, at] for i in range(6) if i != side]
        inner.insert(side, jnp.where(outside, 0.0, w))
        set_weights(at, diag[at] + w, inner)

    for z in [0, depth - 1, *range(1, depth - 1)]:
        lax.fori_loop(0, per_plane, lambda q, _, z=z: (weight_chunk(z, q), 0)[1], 0)
    sig_out.wait_recv()
    sig_share.start()
    sig_share.wait_recv()
    for z in (0, depth - 1):
        lax.fori_loop(0, per_plane, lambda q, _, z=z: (finish_chunk(z, q), 0)[1], 0)
    for copy in load_ints:
        copy.wait()

    def stage(k, c):
        def field(at):
            return x_in[c, at] if k == 0 else v[k - 1, c, at]

        firsts = range(k + 1)
        cell = sources[c, group] - slab * (cells * 128) if k == 0 else None

        def work(row, below, above):
            here = pl.ds(PAD + row, plane)
            at = pl.ds(row, plane)
            mid = field(here)
            image = (
                weights[0, at] * below
                + weights[1, at] * above
                + weights[2, at] * field(pl.ds(PAD - 1 + row, plane))
                + weights[3, at] * field(pl.ds(PAD + 1 + row, plane))
                + weights[4, at] * pltpu.roll(mid, 1, 1)
                + weights[5, at] * pltpu.roll(mid, 127, 1)
            )
            if k == 0:
                ids = (
                    lax.broadcasted_iota(jnp.int32, (plane, 128), 0) + row
                ) * 128 + lax.broadcasted_iota(jnp.int32, (plane, 128), 1)
                new = jnp.where(ids == cell, recip[at], 0.0) + (image - mid)
            else:
                j = k - 1
                new = (1.0 / B[k]) * image + (-A[j] / B[k]) * mid
                if j:
                    new = new + (-B[j] / B[k]) * v[k - 2, c, here]
            v[k, c, here] = new

        def dots(q, sums):
            row = start_row(q)
            here = pl.ds(PAD + row, CHUNK)
            scaled = diag[pl.ds(row, CHUNK)] * v[k, c, here]
            out = []
            for i, total in zip(firsts, sums):
                product = scaled * v[i, c, here]
                for part in range(CHUNK // 8):
                    total = total + product[part * 8:(part + 1) * 8]
                out.append(total)
            return tuple(out)

        def inside(z, _):
            row = pl.multiple_of(z * plane, plane)
            work(row, field(pl.ds(PAD + row - plane, plane)), field(pl.ds(PAD + row + plane, plane)))
            return 0

        lax.fori_loop(1, depth - 1, inside, 0)
        sums = tuple(jnp.zeros((8, 128), jnp.float32) for _ in firsts)
        sums = lax.fori_loop(per_plane, (depth - 1) * per_plane, dots, sums)

        from_left, from_right = halo_copies(k, c)
        to_right, to_left = halo_copies(k + 1, c)
        from_left.wait_recv()
        work(0, halo[k, 0, c], field(pl.ds(PAD + plane, plane)))
        if k == ITERS - 1:
            pl.when((c == 0) | (c == ncol - 1))(lambda: to_left.start())

            @pl.when(c == ncol - 1)
            def _():
                for late in range(1, ncol - 1):
                    halo_copies(k + 1, late)[1].start()

        else:
            to_left.start()
        from_right.wait_recv()
        work(cells - plane, field(pl.ds(PAD + cells - 2 * plane, plane)), halo[k, 1, c])
        to_right.start()

        sums = lax.fori_loop(0, per_plane, dots, sums)
        sums = lax.fori_loop((depth - 1) * per_plane, depth * per_plane, dots, sums)
        for i, total in zip(firsts, sums):
            row = jnp.sum(total, axis=0, keepdims=True)
            rows_acc[pl.ds(SLOT[i, k] * ncol + c, 1), :] = row

    def fold(array):
        total = array[0:8]
        for part in range(8, plane, 8):
            total = total + array[part:part + 8]
        return total

    def last_plane(c, row, below, above):
        here, at = pl.ds(PAD + row, plane), pl.ds(row, plane)
        mid = v[ITERS - 1, c, here]
        image = (
            weights[2, at] * v[ITERS - 1, c, pl.ds(PAD - 1 + row, plane)]
            + weights[3, at] * v[ITERS - 1, c, pl.ds(PAD + 1 + row, plane)]
            + weights[4, at] * pltpu.roll(mid, 1, 1)
            + weights[5, at] * pltpu.roll(mid, 127, 1)
        )
        if below:
            image = image + weights[0, at] * v[ITERS - 1, c, pl.ds(PAD + row - plane, plane)]
        if above:
            image = image + weights[1, at] * v[ITERS - 1, c, pl.ds(PAD + row + plane, plane)]
        v[ITERS, c, here] = (
            (1.0 / B[ITERS]) * image
            + (-A[ITERS - 1] / B[ITERS]) * mid
            + (-B[ITERS - 1] / B[ITERS]) * v[ITERS - 2, c, here]
        )
        held_acc[c] = held_acc[c] + fold(diag[at] * mid * image)

    def last_inner(c, _):
        held_acc[c] = jnp.zeros((8, 128), jnp.float32)
        last_plane(c, 0, False, True)

        def inside(z, _):
            last_plane(c, pl.multiple_of(z * plane, plane), True, True)
            return 0

        lax.fori_loop(1, depth - 1, inside, 0)
        last_plane(c, cells - plane, True, False)
        return 0

    def last_edge(c, side, summed):
        halo_copies(ITERS, c)[side].wait_recv()
        row = 0 if side == 0 else cells - plane
        here, at = pl.ds(PAD + row, plane), pl.ds(row, plane)
        outer = weights[side, at] * halo[ITERS, side, c]
        v[ITERS, c, here] = v[ITERS, c, here] + (1.0 / B[ITERS]) * outer
        if summed:
            total = held_acc[c] + 2.0 * fold(diag[at] * v[ITERS - 1, c, here] * outer)
            last_acc[pl.ds(c, 1), :] = jnp.sum(total, axis=0, keepdims=True)

    reach = [4]
    while 2 * reach[-1] < slabs:
        reach.append(2 * reach[-1])
    rounds = reach[:-1]

    for k in range(STAGES):
        at_round = k - 4
        if 1 <= at_round <= len(rounds):
            for side in range(2):
                pl.semaphore_wait(known_sem.at[at_round - 1, side], 1)
        if 0 <= at_round < len(rounds):
            for side, far in enumerate((rounds[at_round], slabs - rounds[at_round])):
                pl.semaphore_signal(
                    known_sem.at[at_round, side], inc=1,
                    device_id=((slab + far) % slabs, group), device_id_type=MESH,
                )
        if k == ITERS:
            mine = jnp.sum(jnp.transpose(rows_acc[...]), axis=0, keepdims=True)
            lax.fori_loop(0, ncol, last_inner, 0)
            lax.fori_loop(0, ncol - 1, lambda c, _: (last_edge(c, 0, True), 0)[1], 0)
            last_edge(ncol - 1, 1, True)
            break

        def column(c, _, k=k):
            if k == 0:
                pltpu.make_async_copy(x_hbm.at[c], x_in.at[c, body], load_sem.at[1 + c]).wait()
            stage(k, c)
            return 0

        lax.fori_loop(0, ncol, column, 0)

    spot = SLOT[ITERS - 1, ITERS] * ncol + lax.broadcasted_iota(jnp.int32, (8, 128), 0)
    last = jnp.where(
        lax.broadcasted_iota(jnp.int32, (8, 128), 1) == spot, jnp.sum(last_acc[...], axis=1, keepdims=True), 0.0
    )
    parts[slab] = mine + jnp.sum(last, axis=0, keepdims=True)
    part_copies = [remote(parts.at[slab], parts.at[slab], part_send, part_recv, at) for at in others]
    for copy in part_copies:
        copy.start()
    last_edge(ncol - 1, 0, False)
    lax.fori_loop(0, ncol - 1, lambda c, _: (last_edge(c, 1, False), 0)[1], 0)
    sig_out.wait_send()
    sig_share.wait_send()
    for k in range(STAGES):
        def sent(c, _, k=k):
            for copy in halo_copies(k, c):
                copy.wait_send()
            return 0

        lax.fori_loop(0, ncol, sent, 0)
    every = parts.at[pl.ds(0, slabs - 1)]
    all_parts = remote(every, every, part_send, part_recv, right)
    all_parts.wait_recv()
    terms = [parts[i] for i in range(slabs)]
    while len(terms) > 1:
        terms = [sum(terms[i:i + 2][1:], terms[i]) for i in range(0, len(terms), 2)]
    total = terms[0]

    wide = jnp.broadcast_to(total, (8, 128))
    entries = {}
    for pair, at in SLOT.items():
        entries[pair] = wide if at == 0 else pltpu.roll(wide, 128 - at * ncol, 1)

    entries[(ITERS - 1, ITERS)] = (
        entries[(ITERS - 1, ITERS)]
        - A[ITERS - 1] * entries[(ITERS - 1, ITERS - 1)]
        - B[ITERS - 1] * entries[(ITERS - 2, ITERS - 1)]
    ) / B[ITERS]

    def gram(i, j):
        return entries[(i, j)] if i <= j and (i, j) in entries else entries[(j, i)]

    c_x, c_r = coefficients(gram)
    live = lax.broadcasted_iota(jnp.int32, (8, 128), 1) < counts[group]
    for j, value in enumerate(c_x + c_r):
        value = jnp.where(live, value, 0.0)
        for c in range(ncol):
            table[c, pl.ds(j, 1)] = jnp.broadcast_to(value[:1, c:c + 1], (1, 128))

    all_parts.wait_send()


def combine_kernel(dims, x_in, v, diag, table, pot_hbm, res_hbm, pot, res, out_sem):
    ncol, cells, plane = dims

    def out_copies(c, row):
        at = pl.ds(row, plane)
        return (
            pltpu.make_async_copy(pot.at[c, at], pot_hbm.at[c, at], out_sem.at[0, c, row // plane]),
            pltpu.make_async_copy(res.at[c, at], res_hbm.at[c, at], out_sem.at[1, c, row // plane]),
        )

    for c in range(ncol):
        def combine(z, _, c=c):
            row = pl.multiple_of(z * plane, plane)
            here, at = pl.ds(PAD + row, plane), pl.ds(row, plane)
            new_x, new_r = x_in[c, here], None
            for j in range(STAGES):
                vec = v[j, c, here]
                if j < ITERS:
                    new_x = new_x + table[c, pl.ds(j, 1)] * vec
                term = table[c, pl.ds(ITERS + j, 1)] * vec
                new_r = term if new_r is None else new_r + term
            pot[c, at] = new_x
            res[c, at] = diag[at] * new_r
            for copy in out_copies(c, row):
                copy.start()
            return 0

        lax.fori_loop(0, cells // plane, combine, 0)
    for c in range(ncol):
        for row in range(0, cells, plane):
            for copy in out_copies(c, row):
                copy.wait()


def solution(mesh):
    slabs = mesh.shape["slab"]

    def shards(sigma, iterate, counts, sources):
        depth, rows, lanes = sigma.shape
        ncol = iterate.shape[0]
        cells = depth * rows
        f32 = jnp.float32
        vmem = pltpu.VMEM
        dma = pltpu.SemaphoreType.DMA
        anywhere = pl.BlockSpec(memory_space=pl.ANY)
        on_chip = pl.BlockSpec(memory_space=pltpu.VMEM)

        def in_hbm(array):
            return pltpu.with_memory_space_constraint(array, pltpu.HBM)

        sources = sources.T
        held = pl.pallas_call(
            functools.partial(basis_kernel, (slabs, ncol, depth, rows)),
            out_shape=(
                vmem((ncol, cells + 2 * PAD, lanes), f32),
                vmem((STAGES, ncol, cells + 2 * PAD, lanes), f32),
                vmem((cells, lanes), f32),
                vmem((ncol, 16, lanes), f32),
            ),
            in_specs=[anywhere] * 4,
            out_specs=(on_chip,) * 4,
            scratch_shapes=[
                pltpu.SMEM(counts.shape, jnp.int32),
                pltpu.SMEM(sources.shape, jnp.int32),
                vmem((cells + 2 * PAD, lanes), f32),
                vmem((STAGES, 2, ncol, rows, lanes), f32),
                vmem((2, rows, lanes), f32),
                vmem((6, cells, lanes), f32),
                vmem((cells, lanes), f32),
                vmem((128, 128), f32),
                vmem((8, 128), f32),
                vmem((ncol, 8, 128), f32),
                vmem((slabs, 1, 128), f32),
                dma((3 + ncol,)),
                dma((2,)),
                dma((2,)),
                dma((STAGES, 2, ncol)),
                dma((STAGES, 2, ncol)),
                dma,
                dma,
                pltpu.SemaphoreType.REGULAR((2, 2)),
            ],
            compiler_params=pltpu.CompilerParams(
                collective_id=0, has_side_effects=True, vmem_limit_bytes=24 * 1024 * 1024
            ),
        )(
            in_hbm(counts),
            in_hbm(sources),
            in_hbm(sigma.reshape(cells, lanes)),
            in_hbm(iterate.reshape(ncol, cells, lanes)),
        )
        flat = pltpu.HBM((ncol, cells, lanes), f32)
        potential, residual = pl.pallas_call(
            functools.partial(combine_kernel, (ncol, cells, rows)),
            out_shape=(flat, flat),
            in_specs=[on_chip] * 4,
            out_specs=(anywhere, anywhere),
            scratch_shapes=[vmem((ncol, cells, lanes), f32), vmem((ncol, cells, lanes), f32), dma((2, ncol, depth))],
            compiler_params=pltpu.CompilerParams(vmem_limit_bytes=24 * 1024 * 1024),
        )(*held)
        return potential.reshape(iterate.shape), residual.reshape(iterate.shape)

    return jax.shard_map(
        shards,
        mesh=mesh,
        in_specs=(P("slab", None, None), P("src", "slab", None, None), P(), P()),
        out_specs=(P("src", "slab", None, None), P("src", "slab", None, None)),
        check_vma=False,
    )
```
